32 devices in a mesh: dp: 8 (over z, y), tensor: 4 (over x, core).
Axes of the slice: x: 2, y: 2, z: 4, core: 2. Of those that a mesh axis runs over, the one named last changes fastest.
Arguments:
- tokens: bfloat16 [8192, 1280], P(('dp', 'tensor')), may hold values from -6 to 6
- lengths: int32 [8], P('dp'), may hold values from 200 to 1024, as said below
- gain_one: float32 [1280], replicated, may hold values from 0.5 to 1.5
- shift_one: float32 [1280], replicated, may hold values from -1.75 to 1.75
- weight_in: bfloat16 [1280, 3, 1280], P(None, None, 'tensor'), may hold values from -0.15625 to 0.15625
- bias_in: float32 [2, 1280], P(None, 'tensor'), may hold values from -3 to 3
- weight_out: bfloat16 [1280, 1280], P('tensor'), may hold values from -1 to 1
- bias_out: float32 [1280], replicated, may hold values from -1.75 to 1.75
- gain_two: float32 [1280], replicated, may hold values from 0.5 to 1.5
- shift_two: float32 [1280], replicated, may hold values from -1.75 to 1.75
- weight_up: bfloat16 [1280, 5120], P(None, 'tensor'), may hold values from -0.15625 to 0.15625
- bias_up: float32 [5120], P('tensor'), may hold values from -3 to 3
- weight_down: bfloat16 [5120, 1280], P('tensor'), may hold values from -0.078125 to 0.078125
- bias_down: float32 [1280], replicated, may hold values from -1.75 to 1.75
- cotangent: bfloat16 [8192, 1280], P(('dp', 'tensor')), may hold values from -6 to 6
Outputs:
- layer_output: float32 [8192, 1280], P(('dp', 'tensor'))
- grad_tokens: float32 [8192, 1280], P(('dp', 'tensor'))
- grad_gain_one: float32 [1280], replicated
- grad_shift_one: float32 [1280], replicated
- grad_weight_in: float32 [1280, 3, 1280], P(None, None, 'tensor')
- grad_bias_in: float32 [2, 1280], P(None, 'tensor')
- grad_weight_out: float32 [1280, 1280], P('tensor')
- grad_bias_out: float32 [1280], replicated
- grad_gain_two: float32 [1280], replicated
- grad_shift_two: float32 [1280], replicated
- grad_weight_up: float32 [1280, 5120], P(None, 'tensor')
- grad_bias_up: float32 [5120], P('tensor')
- grad_weight_down: float32 [5120, 1280], P('tensor')
- grad_bias_down: float32 [1280], replicated
The draws below stay inside these ranges and needn't reach their ends.
Inputs may be any that keep to these rules, and one draw needn't show every extreme that they name: Sentence s uses slots 0 to lengths[s] - 1; some sentence uses all 1024 slots and some uses the fewest allowed.
All inputs are finite; a program needn't handle non-finite values.
Results may differ from the reference program's by a relative error of at most 0.011.
Values may be sent and summed in bfloat16 or wider, within the bound.
A program may use at most 128 MiB of HBM per device.

```python
import jax
import jax.numpy as jnp
from jax import lax

D = 1280
H = 20
HD = 64
FF = 5120
LEN = 1024
SEQ_DEV = 1
SEQS = 8
TOKENS = 8192
N_DP = 8


def draw_lengths(key, part):
    shortest = LEN * 25 // 128
    base = jax.random.randint(jax.random.fold_in(key, 11), (SEQS,), shortest, LEN + 1)
    where_full = jax.random.randint(jax.random.fold_in(key, 12), (), 0, SEQS)
    where_short = (where_full + 1) % SEQS
    positions = jnp.arange(SEQS)
    base = jnp.where(positions == where_full, LEN, base)
    base = jnp.where(positions == where_short, shortest, base)
    return base.astype(jnp.int32)


def block_levels(key, shape, split, low, top_value):
    def one(axis_at, blocks):
        draws = jax.random.uniform(jax.random.fold_in(jax.random.fold_in(key, 6), axis_at), (blocks,), jnp.float32, low / len(split), top_value / len(split))
        return jnp.repeat(jnp.exp(draws), shape[axis_at] // blocks).reshape((-1,) + (1,) * (len(shape) - axis_at - 1))

    factor_of = one(*split[0])
    for cut in split[1:]:
        factor_of = factor_of * one(*cut)
    return factor_of


def centred(stream_key, shape, scale, reach, shards=(), held_as=jnp.bfloat16):
    factor_of = block_levels(stream_key, shape, shards, -0.22, 0.18) if shards else 1.0
    array = jax.random.normal(stream_key, shape, jnp.float32) * scale * factor_of
    return jnp.minimum(jnp.maximum(array, -reach), reach).astype(held_as)


def setup_inputs(seed: int = 0) -> dict:
    key_list = jax.random.split(jax.random.key(seed), 16)
    return {
        "tokens": centred(key_list[0], (TOKENS, D), 1.0, 6.0, ((0, 32),)),
        "lengths": draw_lengths(jax.random.fold_in(key_list[15], 71), 0),
        "gain_one": jnp.clip(1.0 + 0.1 * jax.random.normal(key_list[2], (D,), jnp.float32), 0.5, 1.5),
        "shift_one": centred(key_list[3], (D,), 0.3, 1.75, (), jnp.float32),
        "weight_in": centred(key_list[4], (D, 3, H * HD), D ** -0.5, 0.15625, ((2, 4),)),
        "bias_in": centred(key_list[5], (2, H * HD), 0.5, 3.0, ((1, 4),), jnp.float32),
        "weight_out": centred(key_list[6], (H * HD, D), (H * HD // 32) ** -0.5, 1.0, ((0, 4),)),
        "bias_out": centred(key_list[7], (D,), 0.3, 1.75, (), jnp.float32),
        "gain_two": jnp.clip(1.0 + 0.1 * jax.random.normal(key_list[8], (D,), jnp.float32), 0.5, 1.5),
        "shift_two": centred(key_list[9], (D,), 0.3, 1.75, (), jnp.float32),
        "weight_up": centred(key_list[10], (D, FF), D ** -0.5, 0.15625, ((1, 4),)),
        "bias_up": centred(key_list[11], (FF,), 0.5, 3.0, ((0, 4),), jnp.float32),
        "weight_down": centred(key_list[12], (FF, D), FF ** -0.5, 0.078125, ((0, 4),)),
        "bias_down": centred(key_list[13], (D,), 0.3, 1.75, (), jnp.float32),
        "cotangent": centred(key_list[14], (TOKENS, D), 1.0, 6.0, ((0, 32),)),
    }


@jax.custom_vjp
def low(v):
    return lax.optimization_barrier(v.astype(jnp.bfloat16)).astype(jnp.float32)

@jax.custom_vjp
def low_back(v):
    return v

def low_keep(v):
    return (low(v), None)

def low_pass(kept, grad):
    return (grad,)

def back_keep(v):
    return (v, None)

def back_low(kept, grad):
    return (low(grad),)
low.defvjp(low_keep, low_pass)
low_back.defvjp(back_keep, back_low)

def normalize(rows, gain, shift):
    centre = rows - lax.optimization_barrier(jnp.mean(rows, axis=-1, keepdims=True))
    spread = lax.optimization_barrier(jnp.mean(centre * centre, axis=-1, keepdims=True))
    return centre * lax.rsqrt(spread + 1e-05) * gain + shift

def matmul(left, right):
    return jnp.dot(left, right, precision=lax.Precision.HIGHEST)

def attend(query_seq, key_seq, value_seq, length):
    scores = jnp.einsum('qhd,khd->hqk', query_seq, key_seq, precision=lax.Precision.HIGHEST) * HD ** (-0.5)
    scores = low_back(scores)
    valid = jnp.arange(LEN) < length
    masked = jnp.where(valid[None, None, :], scores, -1e+30)
    top = lax.optimization_barrier(jnp.max(masked, axis=-1, keepdims=True))
    weights = jnp.exp(masked - top)
    probs = weights / lax.optimization_barrier(jnp.sum(weights, axis=-1, keepdims=True))
    return jnp.einsum('hqk,khd->qhd', low(probs), value_seq, precision=lax.Precision.HIGHEST)

def attend_item(item):
    return attend(item[0], item[1], item[2], item[3])

def layer(rows, params, group_lengths):
    gain_one, shift_one, weight_in, bias_in, weight_out, bias_out, gain_two, shift_two, weight_up, bias_up, weight_down, bias_down = params
    width = H * HD
    first = low(normalize(rows, gain_one, shift_one))
    mixed = matmul(first, weight_in.reshape(D, 3 * width)).reshape(-1, 3, width)
    query_rows = low_back(low(mixed[:, 0] + bias_in[0]))
    key_rows = low_back(low(mixed[:, 1]))
    value_rows = low_back(low(mixed[:, 2] + bias_in[1]))
    shape_seq = (SEQ_DEV, LEN, H, HD)
    context = lax.map(jax.checkpoint(attend_item), (query_rows.reshape(shape_seq), key_rows.reshape(shape_seq), value_rows.reshape(shape_seq), group_lengths))
    context = low_back(low(context.reshape(-1, width)))
    branch = low_back(matmul(context, weight_out) + bias_out)
    middle = rows + branch
    second = low(normalize(middle, gain_two, shift_two))
    hidden = low_back(matmul(second, weight_up) + bias_up)
    active = low(jax.nn.gelu(hidden, approximate=False))
    return middle + matmul(active, weight_down) + bias_down

def reference(tokens, lengths, gain_one, shift_one, weight_in, bias_in, weight_out, bias_out, gain_two, shift_two, weight_up, bias_up, weight_down, bias_down, cotangent):
    params = (gain_one, shift_one, weight_in, bias_in, weight_out, bias_out, gain_two, shift_two, weight_up, bias_up, weight_down, bias_down)
    params = tuple((item.astype(jnp.float32) for item in params))
    rows_all = tokens.astype(jnp.float32).reshape(N_DP, SEQ_DEV * LEN, D)
    lengths_all = lengths.reshape(N_DP, SEQ_DEV)
    cot_all = cotangent.astype(jnp.float32).reshape(N_DP, SEQ_DEV * LEN, D)

    def group(totals, item):
        rows, group_lengths, cot = item
        result, pull = jax.vjp(lambda here, weights: layer(here, weights, group_lengths), rows, params)
        grad_rows, grad_params = pull(cot)
        totals = tuple((left + right for left, right in zip(totals, grad_params)))
        return (totals, (result, grad_rows))
    zeros = tuple((jnp.zeros_like(item) for item in params))
    totals, (results, grads) = lax.scan(group, zeros, (rows_all, lengths_all, cot_all))
    return (results.reshape(TOKENS, D), grads.reshape(TOKENS, D), totals[0], totals[1], totals[2], totals[3], totals[4], totals[5], totals[6], totals[7], totals[8], totals[9], totals[10], totals[11])
```

```python
import jax
import jax.numpy as jnp
from jax import lax
from jax.sharding import PartitionSpec as P

HD = 64
LEN = 1024


def normalize(rows, gain, shift):
    centre = rows - jnp.mean(rows, axis=-1, keepdims=True)
    spread = jnp.mean(centre * centre, axis=-1, keepdims=True)
    return centre * lax.rsqrt(spread + 1e-05) * gain + shift


def masked_scores(query_block, key_seq, length):
    scores = jnp.einsum(
        "qhd,khd->hqk", query_block, key_seq, preferred_element_type=jnp.float32
    ) * HD ** (-0.5)
    valid = jnp.arange(LEN) < length
    return jnp.where(valid[None, None, :], scores, -1e30)


def forward_block(query_block, key_seq, value_seq, length):
    masked = masked_scores(query_block, key_seq, length)
    top = jnp.max(masked, axis=-1, keepdims=True)
    weights = jnp.exp(masked - top)
    total = jnp.sum(weights, axis=-1, keepdims=True)
    probs = (weights / total).astype(jnp.bfloat16)
    context = jnp.einsum("hqk,khd->qhd", probs, value_seq, preferred_element_type=jnp.float32)
    return (context, top[..., 0] + jnp.log(total[..., 0]))


def forward_sequence(item):
    query_seq, key_seq, value_seq, length = item
    return lax.map(
        lambda query_block: forward_block(query_block, key_seq, value_seq, length), query_seq
    )


def backward_sequence(item):
    query_seq, key_seq, value_seq, grad_seq, log_seq, length = item

    def step(carry, inner):
        key_total, value_total = carry
        query_block, grad_block, log_block = inner
        masked = masked_scores(query_block, key_seq, length)
        probs = jnp.exp(masked - log_block[..., None])
        grad_probs = jnp.einsum(
            "qhd,khd->hqk", grad_block, value_seq, preferred_element_type=jnp.float32
        )
        inner_sum = jnp.sum(grad_probs * probs, axis=-1, keepdims=True)
        grad_scores = (probs * (grad_probs - inner_sum)).astype(jnp.bfloat16)
        query_grad = (
            jnp.einsum("hqk,khd->qhd", grad_scores, key_seq, preferred_element_type=jnp.float32)
            * HD ** (-0.5)
        ).astype(jnp.bfloat16)
        key_total = key_total + jnp.einsum(
            "hqk,qhd->khd", grad_scores, query_block, preferred_element_type=jnp.float32
        ) * HD ** (-0.5)
        value_total = value_total + jnp.einsum(
            "hqk,qhd->khd",
            probs.astype(jnp.bfloat16),
            grad_block,
            preferred_element_type=jnp.float32,
        )
        return ((key_total, value_total), query_grad)

    zero_state = jnp.zeros(key_seq.shape, jnp.float32)
    (key_total, value_total), query_grads = lax.scan(
        step, (zero_state, zero_state), (query_seq, grad_seq, log_seq)
    )
    return (query_grads, key_total.astype(jnp.bfloat16), value_total.astype(jnp.bfloat16))


def sum_dp(part):
    return lax.psum(part.astype(jnp.bfloat16), "dp").astype(jnp.float32)


def local(
    tokens,
    lengths,
    gain_one,
    shift_one,
    weight_in,
    bias_in,
    weight_out,
    bias_out,
    gain_two,
    shift_two,
    weight_up,
    bias_up,
    weight_down,
    bias_down,
    cotangent,
):
    sentences = lengths.shape[0]
    width = weight_in.shape[2]
    heads = width // HD
    block_rows = min(512, LEN)
    blocks = LEN // block_rows
    group_rows = sentences * LEN
    query_shape = (sentences, blocks, block_rows, heads, HD)
    key_shape = (sentences, LEN, heads, HD)
    rows_in = tokens.astype(jnp.float32)
    first_local = normalize(rows_in, gain_one, shift_one).astype(jnp.bfloat16)
    first = lax.all_gather(first_local, "tensor", axis=0, tiled=True)
    mixed = jnp.einsum("rd,dcw->rcw", first, weight_in, preferred_element_type=jnp.float32)
    query_rows = (mixed[:, 0] + bias_in[0]).astype(jnp.bfloat16).reshape(query_shape)
    key_rows = mixed[:, 1].astype(jnp.bfloat16).reshape(key_shape)
    value_rows = (mixed[:, 2] + bias_in[1]).astype(jnp.bfloat16).reshape(key_shape)
    context, log_totals = lax.map(forward_sequence, (query_rows, key_rows, value_rows, lengths))
    context_rows = context.reshape(group_rows, width).astype(jnp.bfloat16)
    middle = rows_in + (
        lax.psum_scatter(
            jnp.dot(context_rows, weight_out, preferred_element_type=jnp.float32).astype(jnp.bfloat16),
            "tensor",
            scatter_dimension=0,
            tiled=True,
        ).astype(jnp.float32)
        + bias_out
    )
    second_local = normalize(middle, gain_two, shift_two).astype(jnp.bfloat16)
    second = lax.all_gather(second_local, "tensor", axis=0, tiled=True)
    hidden = jnp.dot(second, weight_up, preferred_element_type=jnp.float32) + bias_up
    active = jax.nn.gelu(hidden, approximate=False).astype(jnp.bfloat16)
    layer_output = (
        middle
        + lax.psum_scatter(
            jnp.dot(active, weight_down, preferred_element_type=jnp.float32).astype(jnp.bfloat16),
            "tensor",
            scatter_dimension=0,
            tiled=True,
        ).astype(jnp.float32)
        + bias_down
    )
    grad_out = cotangent.astype(jnp.float32)
    grad_bias_down = jnp.sum(grad_out, axis=0)
    cot_group = lax.all_gather(cotangent, "tensor", axis=0, tiled=True)
    grad_weight_down = jnp.einsum(
        "rf,rd->fd", active, cot_group, preferred_element_type=jnp.float32
    )
    grad_active = jnp.einsum(
        "rd,fd->rf", cot_group, weight_down, preferred_element_type=jnp.float32
    )
    before_gelu = jnp.dot(second, weight_up, preferred_element_type=jnp.float32) + bias_up
    unused, gelu_pull = jax.vjp(lambda value: jax.nn.gelu(value, approximate=False), before_gelu)
    grad_hidden = gelu_pull(grad_active)[0].astype(jnp.bfloat16)
    grad_weight_up = jnp.einsum(
        "rd,rf->df", second, grad_hidden, preferred_element_type=jnp.float32
    )
    grad_bias_up = jnp.sum(grad_hidden.astype(jnp.float32), axis=0)
    grad_second = lax.psum_scatter(
        jnp.einsum("rf,df->rd", grad_hidden, weight_up, preferred_element_type=jnp.float32).astype(jnp.bfloat16),
        "tensor",
        scatter_dimension=0,
        tiled=True,
    ).astype(jnp.float32)
    unused_two, second_pull = jax.vjp(normalize, middle, gain_two, shift_two)
    middle_part, grad_gain_two, grad_shift_two = second_pull(grad_second)
    grad_middle = grad_out + middle_part
    grad_branch = grad_middle.astype(jnp.bfloat16)
    grad_bias_out = jnp.sum(grad_branch.astype(jnp.float32), axis=0)
    branch_group = lax.all_gather(grad_branch, "tensor", axis=0, tiled=True)
    grad_weight_out = jnp.einsum(
        "rw,rd->wd", context_rows, branch_group, preferred_element_type=jnp.float32
    )
    grad_context = jnp.einsum(
        "rd,wd->rw", branch_group, weight_out, preferred_element_type=jnp.float32
    ).astype(jnp.bfloat16)
    query_grads, key_grads, value_grads = lax.map(
        backward_sequence,
        (query_rows, key_rows, value_rows, grad_context.reshape(query_shape), log_totals, lengths),
    )
    query_flat = query_grads.reshape(group_rows, width)
    value_flat = value_grads.reshape(group_rows, width)
    grad_mixed = jnp.stack([query_flat, key_grads.reshape(group_rows, width), value_flat], axis=1)
    grad_weight_in = jnp.einsum(
        "rd,rcw->dcw", first, grad_mixed, preferred_element_type=jnp.float32
    )
    grad_bias_in = jnp.stack(
        [
            jnp.sum(query_flat.astype(jnp.float32), axis=0),
            jnp.sum(value_flat.astype(jnp.float32), axis=0),
        ]
    )
    grad_first = lax.psum_scatter(
        jnp.einsum("rcw,dcw->rd", grad_mixed, weight_in, preferred_element_type=jnp.float32).astype(jnp.bfloat16),
        "tensor",
        scatter_dimension=0,
        tiled=True,
    ).astype(jnp.float32)
    unused_one, first_pull = jax.vjp(normalize, rows_in, gain_one, shift_one)
    rows_part, grad_gain_one, grad_shift_one = first_pull(grad_first)
    grad_tokens = grad_middle + rows_part
    grad_bias_in, grad_bias_up = lax.psum((grad_bias_in, grad_bias_up), "dp")
    grad_weight_in = sum_dp(grad_weight_in)
    grad_weight_out = sum_dp(grad_weight_out)
    grad_weight_up = sum_dp(grad_weight_up)
    grad_weight_down = sum_dp(grad_weight_down)
    grad_gain_one, grad_shift_one, grad_bias_out, grad_gain_two, grad_shift_two, grad_bias_down = (
        lax.psum(
            (
                grad_gain_one,
                grad_shift_one,
                grad_bias_out,
                grad_gain_two,
                grad_shift_two,
                grad_bias_down,
            ),
            ("dp", "tensor"),
        )
    )
    return (
        layer_output,
        grad_tokens,
        grad_gain_one,
        grad_shift_one,
        grad_weight_in,
        grad_bias_in,
        grad_weight_out,
        grad_bias_out,
        grad_gain_two,
        grad_shift_two,
        grad_weight_up,
        grad_bias_up,
        grad_weight_down,
        grad_bias_down,
    )


def solution(mesh):
    placed = (
        P(("dp", "tensor"), None),
        P("dp"),
        P(),
        P(),
        P(None, None, "tensor"),
        P(None, "tensor"),
        P("tensor", None),
        P(),
        P(),
        P(),
        P(None, "tensor"),
        P("tensor"),
        P("tensor", None),
        P(),
        P(("dp", "tensor"), None),
    )
    return jax.shard_map(
        local,
        mesh=mesh,
        in_specs=placed,
        out_specs=(
            P(("dp", "tensor"), None),
            P(("dp", "tensor"), None),
            P(),
            P(),
            P(None, None, "tensor"),
            P(None, "tensor"),
            P("tensor", None),
            P(),
            P(),
            P(),
            P(None, "tensor"),
            P("tensor"),
            P("tensor", None),
            P(),
        ),
        check_vma=False,
    )
```

```python
import functools

import jax
import jax.numpy as jnp
from jax import lax
from jax.experimental import pallas as pl
from jax.experimental.pallas import tpu as pltpu
from jax.sharding import PartitionSpec as P

HD = 64
LEN = 1024
BF = jnp.bfloat16
F32 = jnp.float32
MESH = pl.DeviceIdType.MESH
LOG2E = 1.4426950408889634
LN2 = 0.6931471805599453
UNIT = 256
RING = 10
YH = 64
YF = 32
ZF = 64
ZA0 = 128
ZB0 = 192
KINDS = 11
HIGH = 62 * 2**20


def dot(left, right, left_dim, right_dim):
    return lax.dot_general(
        left, right, (((left_dim,), (right_dim,)), ((), ())), preferred_element_type=F32
    )


def norm_parts(rows):
    centre = rows - jnp.mean(rows, axis=-1, keepdims=True)
    scale = lax.rsqrt(jnp.mean(centre * centre, axis=-1, keepdims=True) + 1e-05)
    return centre * scale, scale


def kernel(n_dp, len_ref, tok, cot, vecs, win_h, wout_h, wup_h, wdown_h,
           lo, gtok, small, gout, first_h,
           win, wout, wup, wdown, first, cotg, sec, act, gh,
           qkv, vt, kt, ctxT, dO, dk, dv, mid, gmid, bias, lse,
           ps, rcv, part, yR, zYA, zYB, zZA, zZB, yZ, smr,
           wsem, ag_s, ag_r, rs_s, rs_r, dp_s, dp_r, out_s, sm_s, sm_r):
    line = n_dp // 2
    width = tok.shape[1]
    rows = tok.shape[0]
    heads = dO.shape[0]
    units = gout.shape[0] // UNIT
    gap = max(0, 2 * line + 2 - RING)
    starts = units + gap * ((units - 1) // RING)
    last = starts + 2 * line + 2
    small_at = last - 2 * line - 2
    branch = first
    first2 = act
    dmx = sec

    g = lax.axis_index("dp")
    t = lax.axis_index("tensor")
    cp = t + 1 - 2 * lax.rem(t, 2)
    xp = lax.rem(t + 2, 4)
    dg = lax.rem(cp + 2, 4)
    y = lax.rem(g, 2)
    zl = lax.div(g, 2)
    chip = lax.div(t, 2)
    core_dev = (g, cp)
    x_dev = (g, xp)
    y_dev = (g + 1 - 2 * y, t)
    up_dev = (g + 2, t)
    dn_dev = (g - 2, t)
    has_up = zl < line - 1
    has_dn = zl > 0

    def blk(b):
        return pl.ds(pl.multiple_of(b * rows, rows), rows)

    def rcopy(src, dst, s_sem, r_sem, dev):
        return pltpu.make_async_remote_copy(
            src_ref=src, dst_ref=dst, send_sem=s_sem, recv_sem=r_sem, device_id=dev, device_id_type=MESH
        )

    loads = [
        pltpu.make_async_copy(win_h, win, wsem.at[0]),
        pltpu.make_async_copy(wout_h, wout, wsem.at[1]),
        pltpu.make_async_copy(wup_h, wup, wsem.at[2]),
        pltpu.make_async_copy(wdown_h, wdown, wsem.at[3]),
    ]
    for item in loads:
        item.start()

    barrier = pltpu.get_barrier_semaphore()
    for dev in (core_dev, x_dev, y_dev):
        pl.semaphore_signal(barrier, inc=1, device_id=dev, device_id_type=MESH)

    @pl.when(has_up)
    def _():
        pl.semaphore_signal(barrier, inc=1, device_id=up_dev, device_id_type=MESH)

    @pl.when(has_dn)
    def _():
        pl.semaphore_signal(barrier, inc=1, device_id=dn_dev, device_id_type=MESH)

    class Gather:
        def __init__(self, buf, at):
            own, theirs = buf.at[blk(t), :], buf.at[blk(xp), :]
            self.x = rcopy(own, own, ag_s.at[at, 0], ag_r.at[at, 0], x_dev)
            self.c = rcopy(own, own, ag_s.at[at, 1], ag_r.at[at, 1], core_dev)
            self.f = rcopy(theirs, theirs, ag_s.at[at, 2], ag_r.at[at, 2], core_dev)

        def start(self):
            self.x.start()
            self.c.start()

        def drain(self):
            self.x.wait_send()
            self.c.wait_send()
            self.f.wait_send()

        def near(self):
            self.c.wait_recv()

        def far(self):
            self.x.wait_recv()
            self.f.start()

        def diag(self):
            self.f.wait_recv()

    class Scatter:
        def __init__(self, at, slot):
            self.own_in, self.x_relay, self.x_in = (rcv.at[slot, i] for i in range(3))
            self.d = rcopy(ps.at[0], rcv.at[slot, 1], rs_s.at[at, 0], rs_r.at[at, 0], core_dev)
            self.x = rcopy(ps.at[1], rcv.at[slot, 2], rs_s.at[at, 1], rs_r.at[at, 1], x_dev)
            self.c = rcopy(ps.at[2], rcv.at[slot, 0], rs_s.at[at, 2], rs_r.at[at, 2], core_dev)

        def far(self, fn):
            fn(dg, functools.partial(self.put, 0))
            self.d.start()
            fn(xp, functools.partial(self.put, 1))
            self.d.wait_recv()

            def add(i, _):
                r = pl.ds(pl.multiple_of(i * 64, 64), 64)
                ps[1, r, :] = (ps[1, r, :].astype(F32) + self.x_relay[r, :].astype(F32)).astype(BF)
                return 0

            lax.fori_loop(0, rows // 64, add, 0)
            self.x.start()

        @staticmethod
        def put(slot, cols, value):
            ps[slot, :, cols] = value.astype(BF)

        def close(self, fn, total):
            fn(cp, functools.partial(self.put, 2))
            self.c.start()

            def keep(cols, value):
                total[:, cols] = value

            fn(t, keep)

        def wait(self):
            self.c.wait_recv()
            self.x.wait_recv()

        def extra(self, r):
            return self.own_in[r, :].astype(F32) + self.x_in[r, :].astype(F32)

        def drain(self):
            self.d.wait_send()
            self.x.wait_send()
            self.c.wait_send()

    def unit_of(m):
        if gap == 0:
            return (m >= 0) & (m < units), m
        late = m >= RING + gap
        u = jnp.where(late, m - gap, m)
        return (m >= 0) & (u < units) & (late | (m < RING)), u

    own_a = pl.multiple_of(y * YH, YH)
    own_b = pl.multiple_of(y * YH + YF, YF)
    other = pl.multiple_of((1 - y) * YH, YH)
    R_OWN, R_OTHER = pl.ds(own_a, YH), pl.ds(other, YH)
    R_YA, R_YB = pl.ds(own_a, YF), pl.ds(own_b, YF)
    R_ZA, R_ZB = pl.ds(ZA0, ZF), pl.ds(ZB0, ZF)

    def dcopy(kind, s, src_rows, dst, dev):
        return rcopy(part.at[s, src_rows, :], dst, dp_s.at[kind, s], dp_r.at[kind, s], dev)

    def c_y(s):
        return dcopy(0, s, R_OTHER, yR.at[s], y_dev)

    def c_ya(s):
        return dcopy(1, s, R_YA, zYA.at[s], dn_dev)

    def c_yb(s):
        return dcopy(2, s, R_YB, zYB.at[s], up_dev)

    def c_za(s):
        return dcopy(3, s, R_ZA, zZA.at[s], dn_dev)

    def c_zb(s):
        return dcopy(4, s, R_ZB, zZB.at[s], up_dev)

    def c_ex(s, which):
        return dcopy(5, s, which, yZ.at[s], y_dev)

    def b_ya(s):
        return dcopy(6, s, R_YA, zYA.at[s], up_dev)

    def b_yb(s):
        return dcopy(7, s, R_YB, zYB.at[s], dn_dev)

    def b_y(s):
        return dcopy(8, s, R_OWN, part.at[s, R_OWN, :], y_dev)

    def b_za(s):
        return dcopy(9, s, R_ZA, zZA.at[s], up_dev)

    def b_zb(s):
        return dcopy(10, s, R_ZB, zZB.at[s], dn_dev)

    def add_in(s, where, got):
        part[s, where, :] = (part[s, where, :].astype(F32) + got[s].astype(F32)).astype(BF)

    def out_copy(s, u):
        return pltpu.make_async_copy(
            part.at[s], gout.at[pl.ds(pl.multiple_of(u * UNIT, UNIT), UNIT), :], out_s.at[s]
        )

    def on(m, cond, fn):
        ok, u = unit_of(m)
        if cond is not None:
            ok = ok & cond

        @pl.when(ok)
        def _():
            fn(lax.rem(u, RING), u)

    def step(n):
        def begin(s, u):
            c_y(s).start()

            @pl.when(zl == line - 1)
            def _():
                c_za(s).start()

            @pl.when(zl == 0)
            def _():
                c_zb(s).start()

        def pair_sum(s, u):
            c_y(s).wait()
            add_in(s, R_OWN, yR)

            @pl.when(zl == line - 1)
            def _():
                c_ya(s).start()

            @pl.when(zl == 0)
            def _():
                c_yb(s).start()

        def line_zb(s, u):
            c_zb(s).wait_recv()
            add_in(s, R_ZB, zZB)

            @pl.when(has_up)
            def _():
                c_zb(s).start()

            @pl.when(zl == line - 1)
            def _():
                c_ex(s, R_ZB).start()

        def line_za(s, u):
            c_za(s).wait_recv()
            add_in(s, R_ZA, zZA)

            @pl.when(has_dn)
            def _():
                c_za(s).start()

            @pl.when(zl == 0)
            def _():
                c_ex(s, R_ZA).start()

        def pair_za(s, u):
            c_ex(s, R_ZA).wait()
            add_in(s, R_ZA, yZ)
            b_za(s).start()

        def pair_zb(s, u):
            c_ex(s, R_ZB).wait()
            add_in(s, R_ZB, yZ)
            b_zb(s).start()

        def line_yb(s, u):
            c_yb(s).wait_recv()
            add_in(s, R_YB, zYB)

            @pl.when(has_up)
            def _():
                c_yb(s).start()

            @pl.when(zl == line - 1)
            def _():
                b_yb(s).start()

        def line_ya(s, u):
            c_ya(s).wait_recv()
            add_in(s, R_YA, zYA)

            @pl.when(has_dn)
            def _():
                c_ya(s).start()

            @pl.when(zl == 0)
            def _():
                b_ya(s).start()

        def back_a(s, u):
            c_za(s).wait_send()
            c_ya(s).wait_send()
            b_za(s).wait_recv()
            b_ya(s).wait_recv()
            part[s, R_ZA, :] = zZA[s]
            part[s, R_YA, :] = zYA[s]

            @pl.when(has_up)
            def _():
                b_za(s).start()
                b_ya(s).start()

        def back_b(s, u):
            c_zb(s).wait_send()
            c_yb(s).wait_send()
            b_zb(s).wait_recv()
            b_yb(s).wait_recv()
            part[s, R_ZB, :] = zZB[s]
            part[s, R_YB, :] = zYB[s]

            @pl.when(has_dn)
            def _():
                b_zb(s).start()
                b_yb(s).start()

        def back_pair(s, u):
            b_y(s).start()

        def finish(s, u):
            b_y(s).wait_recv()
            out_copy(s, u).start()

        def drain(s, u):
            out_copy(s, u).wait()
            b_y(s).wait_send()

            @pl.when(has_up)
            def _():
                for item in (b_ya, b_za):
                    item(s).wait_send()

            @pl.when(has_dn)
            def _():
                for item in (b_yb, b_zb):
                    item(s).wait_send()

        on(n, None, begin)
        on(n - 1, None, pair_sum)
        on(n - zl, has_dn, line_zb)
        on(n - (line - 1 - zl), has_up, line_za)
        on(n - line, zl == 0, pair_za)
        on(n - line, zl == line - 1, pair_zb)
        on(n - 1 - zl, has_dn, line_yb)
        on(n - line + zl, has_up, line_ya)
        on(n - line - zl, has_dn, back_a)
        on(n - line - (line - 1 - zl), has_up, back_b)
        on(n - 2 * line + 1, None, back_pair)
        on(n - 2 * line, None, finish)
        on(n - 2 * line - 1, None, drain)

    shared = lax.broadcasted_iota(jnp.int32, (8, width), 0) < 6

    def s_copy(i, src, dst, dev):
        return rcopy(src, dst, sm_s.at[i], sm_r.at[i], dev)

    def small_step(n):
        core = s_copy(0, small, smr.at[0], core_dev)
        across = s_copy(1, small, smr.at[1], x_dev)
        pair = s_copy(2, small, smr.at[2], y_dev)
        down = s_copy(3, small, smr.at[3], dn_dev)
        back = s_copy(4, small, smr.at[4], up_dev)

        def at(m, cond, fn):
            ok = n == small_at + m
            if cond is not None:
                ok = ok & cond
            pl.when(ok)(fn)

        def s0():
            core.start()

        def s1():
            core.wait()
            small[...] = small[...] + jnp.where(shared, smr[0], 0.0)
            across.start()

        def s2():
            across.wait()
            small[...] = small[...] + jnp.where(shared, smr[1], 0.0)
            pair.start()

        def s3():
            pair.wait()
            small[...] = small[...] + smr[2]

            @pl.when(zl == line - 1)
            def _():
                down.start()

        def s4():
            down.wait_recv()
            small[...] = small[...] + smr[3]

            @pl.when(has_dn)
            def _():
                down.start()

            @pl.when(zl == 0)
            def _():
                back.start()

        def s5():
            back.wait_recv()

            @pl.when(has_dn & (zl > 0))
            def _():
                down.wait_send()

            small[...] = smr[4]

            @pl.when(has_up)
            def _():
                back.start()

        at(0, None, s0)
        at(1, None, s1)
        at(2, None, s2)
        at(3, None, s3)
        at(3 + line - 1 - zl, has_up, s4)
        at(3 + line - 1 + zl, has_dn, s5)

    def steps(lo_n, hi_n):
        def body(n, _):
            step(n)
            small_step(n)
            return 0

        lax.fori_loop(lo_n, hi_n, body, 0)

    keys = lax.broadcasted_iota(jnp.int32, (LEN, 128), 0)
    bias[...] = jnp.where(keys < len_ref[0], 0.0, -1e30)
    gain_one, shift_one = vecs[0:1, :], vecs[1:2, :]
    gain_two, shift_two = vecs[3:4, :], vecs[4:5, :]
    CH = 32

    def norm_one(i, _):
        r = pl.ds(pl.multiple_of(i * CH, CH), CH)
        n, _s = norm_parts(tok[r, :].astype(F32))
        first[pl.ds(pl.multiple_of(t * rows + i * CH, CH), CH), :] = (n * gain_one + shift_one).astype(BF)
        return 0

    lax.fori_loop(0, rows // CH, norm_one, 0)
    pl.semaphore_wait(barrier, 3 + has_up.astype(jnp.int32) + has_dn.astype(jnp.int32))
    gather_first = Gather(first, 0)
    gather_first.start()
    own_cot = pltpu.make_async_copy(cot, cotg.at[blk(t), :], wsem.at[4])
    own_cot.start()
    loads[0].wait()

    def project(b):
        f = first[blk(b), :]
        for p in range(0, heads, 2):
            count = min(2, heads - p)
            base = 3 * HD * p
            w = 3 * HD * count
            mixed = dot(f, win[base : base + w, :], 1, 1) + vecs[7:8, base : base + w]
            mixed = mixed.astype(BF)
            for j in range(3 * count):
                piece = mixed[:, j * HD : (j + 1) * HD]
                h, which = p + j // 3, j % 3
                qkv[3 * p + j, blk(b), :] = piece
                if which == 1:
                    kt[h, :, blk(b)] = piece.T
                if which == 2:
                    vt[h, :, blk(b)] = piece.T

    project(t)
    gather_first.near()
    project(cp)
    gather_first.far()
    own_cot.wait()
    gather_cot = Gather(cotg, 1)
    gather_cot.start()
    project(xp)
    gather_first.diag()
    project(dg)
    keep_first = pltpu.make_async_copy(first, first_h, wsem.at[5])
    keep_first.start()

    HALF = 2 * rows
    SCALE = HD**-0.5

    def half(i):
        return pl.ds(pl.multiple_of(i * HALF, HALF), HALF)

    def attend(i):
        def head(h, _):
            q = qkv[3 * h, half(i), :]
            k = qkv[3 * h + 1]
            s = dot(k, q, 1, 1) * (SCALE * LOG2E) + bias[:, 0:1]
            top = jnp.max(s, axis=0, keepdims=True)
            p = jnp.exp2(s - top)
            total = jnp.sum(p, axis=0, keepdims=True)
            o = dot(vt[h], p.astype(BF), 1, 0) / total
            ctxT[pl.ds(pl.multiple_of(h * HD, HD), HD), half(i)] = o.astype(BF)
            lse[h, i] = top + jnp.log2(total)
            return 0

        lax.fori_loop(0, heads, head, 0)

    def tiles(n_cols, fn):
        for c0 in range(0, n_cols, 256):
            fn(slice(c0, c0 + 256))

    def project_out(b, put):
        left = ctxT[:, blk(b)]
        tiles(width, lambda c: put(c, dot(left, wout[:, c], 0, 0)))

    loads[1].wait()
    attend(1 - chip)
    sum_out = Scatter(0, 0)
    sum_out.far(project_out)
    attend(chip)
    gather_cot.near()
    gather_cot.far()
    sum_out.close(project_out, mid)
    sum_out.wait()

    def norm_two(i, _):
        r = pl.ds(pl.multiple_of(i * CH, CH), CH)
        v = tok[r, :].astype(F32) + (mid[r, :] + sum_out.extra(r) + vecs[2:3, :])
        mid[r, :] = v
        n, _s = norm_parts(v)
        sec[pl.ds(pl.multiple_of(t * rows + i * CH, CH), CH), :] = (n * gain_two + shift_two).astype(BF)
        return 0

    lax.fori_loop(0, rows // CH, norm_two, 0)
    keep_first.wait()
    gather_first.drain()
    gather_sec = Gather(sec, 2)
    gather_sec.start()
    sum_out.drain()
    gather_cot.diag()
    loads[2].wait()
    loads[3].wait()

    small[...] = jnp.zeros((8, width), F32)
    f_cols = wup.shape[1]

    def feed(b):
        s_in = sec[blk(b), :]
        g_in = cotg[blk(b), :]

        def cols(i, _):
            c = pl.ds(pl.multiple_of(i * 256, 256), 256)
            hid = dot(s_in, wup[:, c], 1, 0) + vecs[6:7, c]
            phi = 0.5 * (1.0 + lax.erf(hid * 0.7071067811865476))
            act[blk(b), c] = (hid * phi).astype(BF)
            slope = phi + hid * (0.3989422804014327 * jnp.exp(hid * hid * -0.5))
            grad = (dot(g_in, wdown[c, :], 1, 1) * slope).astype(BF)
            gh[blk(b), c] = grad
            small[6:7, c] = small[6:7, c] + jnp.sum(grad.astype(F32), axis=0, keepdims=True)
            return 0

        lax.fori_loop(0, f_cols // 256, cols, 0)

    feed(t)
    gather_sec.near()
    feed(cp)
    gather_sec.far()
    feed(xp)
    gather_sec.diag()
    feed(dg)

    def units_tn(u0, count, left, right):
        def body(i, _):
            lhs = left[:, pl.ds(pl.multiple_of(i * UNIT, UNIT), UNIT)]
            tiles(width, lambda c: part.__setitem__((u0 + i, slice(None), c), dot(lhs, right[:, c], 0, 0).astype(BF)))
            return 0

        lax.fori_loop(0, count, body, 0)

    n_down = f_cols // UNIT
    n_up = width // UNIT
    units_tn(0, n_down, act, cotg)
    step(0)

    def back_up(b, put):
        left = gh[blk(b), :]
        tiles(width, lambda c: put(c, dot(left, wup[c, :], 1, 1)))

    sum_sec = Scatter(1, 1)
    sum_sec.far(back_up)
    sum_sec.close(back_up, gmid)
    units_tn(n_down, n_up, sec, gh)
    step(1)
    sum_sec.wait()

    zero_rows = jnp.zeros((1, width), F32)

    def middle_back(i, carry):
        d_gain, d_shift, d_out, d_down = carry
        r = pl.ds(pl.multiple_of(i * CH, CH), CH)
        e = gmid[r, :] + sum_sec.extra(r)
        n, scale = norm_parts(mid[r, :])
        tt = e * gain_two
        inner = (tt - jnp.mean(tt, -1, keepdims=True) - n * jnp.mean(tt * n, -1, keepdims=True)) * scale
        c_rows = cot[r, :].astype(F32)
        gm = c_rows + inner
        gmid[r, :] = gm
        low = gm.astype(BF)
        branch[pl.ds(pl.multiple_of(t * rows + i * CH, CH), CH), :] = low

        def total(v):
            return jnp.sum(v, axis=0, keepdims=True)

        return (
            d_gain + total(e * n), d_shift + total(e), d_out + total(low.astype(F32)), d_down + total(c_rows)
        )

    d_gain, d_shift, d_out, d_down = lax.fori_loop(0, rows // CH, middle_back, (zero_rows,) * 4)
    small[3:4, :] = d_gain
    small[4:5, :] = d_shift
    small[2:3, :] = d_out
    small[5:6, :] = d_down
    gather_branch = Gather(branch, 3)
    gather_branch.start()
    sum_sec.drain()

    def down(b, put):
        left = act[blk(b), :]
        tiles(width, lambda c: put(c, dot(left, wdown[:, c], 1, 0)))

    sum_down = Scatter(2, 0)
    sum_down.far(down)
    sum_down.close(down, lo)
    load_first = pltpu.make_async_copy(first_h, first2, wsem.at[6])
    load_first.start()
    step(2)

    def back_out(b):
        grad = dot(branch[blk(b), :], wout[...], 1, 1).astype(BF)
        for h in range(heads):
            dO[h, blk(b), :] = grad[:, h * HD : (h + 1) * HD]

    back_out(t)
    gather_branch.near()
    back_out(cp)
    gather_branch.far()
    back_out(xp)
    gather_branch.diag()
    back_out(dg)
    step(3)

    def attend_back(h, _):
        k = qkv[3 * h + 1]
        v = qkv[3 * h + 2]
        for i in range(LEN // HALF):
            r = slice(i * HALF, (i + 1) * HALF)
            q = qkv[3 * h, r, :]
            o_grad = dO[h, r, :]
            s = dot(k, q, 1, 1) * (SCALE * LOG2E) + bias[:, 0:1]
            p = jnp.exp2(s - lse[h, i])
            dp = dot(v, o_grad, 1, 1)
            delta = jnp.sum(p * dp, axis=0, keepdims=True)
            ds = (p * (dp - delta)).astype(BF)
            d_v = dot(p.astype(BF), o_grad, 1, 0)
            d_k = dot(ds, q, 1, 0)
            if i == 0:
                dv[...] = d_v
                dk[...] = d_k
            else:
                dv[...] = dv[...] + d_v
                dk[...] = dk[...] + d_k
            d_q = dot(kt[h], ds, 1, 0) * SCALE
            qkv[3 * h, r, :] = d_q.T.astype(BF)
        qkv[3 * h + 1] = (dk[...] * SCALE).astype(BF)
        qkv[3 * h + 2] = dv[...].astype(BF)
        return 0

    lax.fori_loop(0, heads, attend_back, 0)
    step(4)

    def assemble(i, carry):
        r = pl.ds(pl.multiple_of(i * 256, 256), 256)
        for p in range(3 * heads):
            dmx[r, p * HD : (p + 1) * HD] = qkv[p, r, :]
        return carry + jnp.sum(dmx[r, 0 : 3 * heads * HD].astype(F32), axis=0, keepdims=True)

    gather_sec.drain()
    small[7:8, 0 : 3 * heads * HD] = lax.fori_loop(0, LEN // 256, assemble, jnp.zeros((1, 3 * heads * HD), F32))

    def back_first(b, put):
        left = dmx[blk(b), 0 : 3 * heads * HD]
        tiles(width, lambda c: put(c, dot(left, win[:, c], 1, 0)))

    sum_down.drain()
    sum_first = Scatter(3, 1)
    sum_first.far(back_first)
    sum_first.close(back_first, gtok)
    step(5)
    sum_down.wait()

    def finish_out(i, _):
        r = pl.ds(pl.multiple_of(i * CH, CH), CH)
        lo[r, :] = mid[r, :] + lo[r, :] + sum_down.extra(r) + vecs[5:6, :]
        return 0

    lax.fori_loop(0, rows // CH, finish_out, 0)
    sum_first.wait()

    def tokens_back(i, carry):
        d_gain, d_shift = carry
        r = pl.ds(pl.multiple_of(i * CH, CH), CH)
        e = gtok[r, :] + sum_first.extra(r)
        n, scale = norm_parts(tok[r, :].astype(F32))
        tt = e * gain_one
        inner = (tt - jnp.mean(tt, -1, keepdims=True) - n * jnp.mean(tt * n, -1, keepdims=True)) * scale
        gtok[r, :] = gmid[r, :] + inner
        return (
            d_gain + jnp.sum(e * n, axis=0, keepdims=True), d_shift + jnp.sum(e, axis=0, keepdims=True)
        )

    d_gain, d_shift = lax.fori_loop(0, rows // CH, tokens_back, (zero_rows,) * 2)
    small[0:1, :] = d_gain
    small[1:2, :] = d_shift

    steps(6, RING + gap)
    load_first.wait()
    u0 = n_down + n_up
    n_in = (3 * heads * HD) // UNIT

    def prepare(u):
        s = u % RING
        i = u - u0
        if i < n_in:
            lhs = dmx[:, i * UNIT : (i + 1) * UNIT]
            tiles(width, lambda c: part.__setitem__((s, slice(None), c), dot(lhs, first2[:, c], 0, 0).astype(BF)))
            return
        rest = 3 * heads * HD - n_in * UNIT
        if i == n_in and rest:
            lhs = dmx[:, n_in * UNIT : 3 * heads * HD]
            tiles(width, lambda c: part.__setitem__(
                (s, slice(0, rest), c), dot(lhs, first2[:, c], 0, 0).astype(BF)))
            left = ctxT[0 : UNIT - rest, :]
            tiles(width, lambda c: part.__setitem__(
                (s, slice(rest, UNIT), c), dot(left, branch[:, c], 1, 0).astype(BF)))
            return
        o0 = i * UNIT - 3 * heads * HD
        left = ctxT[o0 : o0 + UNIT, :]
        tiles(width, lambda c: part.__setitem__((s, slice(None), c), dot(left, branch[:, c], 1, 0).astype(BF)))

    for u in range(u0, units):
        prepare(u)
        step(u + gap)
    steps(units + gap, last)

    gather_cot.drain()
    gather_branch.drain()
    sum_first.drain()

    @pl.when(has_up)
    def _():
        s_copy(4, small, smr.at[4], up_dev).wait_send()


def solution(mesh):
    n_dp = mesh.shape["dp"]

    def local(tokens, lengths, gain_one, shift_one, weight_in, bias_in, weight_out, bias_out, gain_two, shift_two,
              weight_up, bias_up, weight_down, bias_down, cotangent):
        rows, width = tokens.shape
        cols = weight_in.shape[2]
        heads = cols // HD
        f_cols = weight_up.shape[1]
        w_in = weight_in.reshape(width, 3, heads, HD).transpose(2, 1, 3, 0).reshape(3 * cols, width)
        b_in = jnp.stack([bias_in[0], jnp.zeros_like(bias_in[0]), bias_in[1]]).reshape(3, heads, HD)
        b_in = jnp.pad(b_in.transpose(1, 0, 2).reshape(3 * cols), (0, width - 3 * cols))
        vecs = jnp.stack([gain_one, shift_one, bias_out, gain_two, shift_two, bias_down, bias_up, b_in])
        total = 4 * rows
        g_rows = f_cols + width + 4 * cols
        vm = pl.BlockSpec(memory_space=pltpu.VMEM)
        hb = pl.BlockSpec(memory_space=pl.ANY)
        big = pltpu.VMEM((total, width), BF)
        lo, gtok, small, gout, _first = pl.pallas_call(
            functools.partial(kernel, n_dp),
            out_shape=[
                jax.ShapeDtypeStruct((rows, width), F32),
                jax.ShapeDtypeStruct((rows, width), F32),
                jax.ShapeDtypeStruct((8, width), F32),
                jax.ShapeDtypeStruct((g_rows, width), BF),
                jax.ShapeDtypeStruct((total, width), BF),
            ],
            in_specs=[pl.BlockSpec(memory_space=pltpu.SMEM), vm, vm, vm, hb, hb, hb, hb],
            out_specs=[vm, vm, vm, hb, hb],
            scratch_shapes=[
                pltpu.VMEM((3 * cols, width), BF),
                pltpu.VMEM((cols, width), BF),
                pltpu.VMEM((width, f_cols), BF),
                pltpu.VMEM((f_cols, width), BF),
                big, big, big,
                pltpu.VMEM((total, f_cols), BF),
                pltpu.VMEM((total, f_cols), BF),
                pltpu.VMEM((3 * heads, LEN, HD), BF),
                pltpu.VMEM((heads, HD, LEN), BF),
                pltpu.VMEM((heads, HD, LEN), BF),
                pltpu.VMEM((cols, LEN), BF),
                pltpu.VMEM((heads, LEN, HD), BF),
                pltpu.VMEM((LEN, HD), F32),
                pltpu.VMEM((LEN, HD), F32),
                pltpu.VMEM((rows, width), F32),
                pltpu.VMEM((rows, width), F32),
                pltpu.VMEM((LEN, 128), F32),
                pltpu.VMEM((heads, 2, 1, 2 * rows), F32),
                pltpu.VMEM((3, rows, width), BF),
                pltpu.VMEM((2, 3, rows, width), BF),
                pltpu.VMEM((RING, UNIT, width), BF),
                pltpu.VMEM((RING, YH, width), BF),
                pltpu.VMEM((RING, YF, width), BF),
                pltpu.VMEM((RING, YF, width), BF),
                pltpu.VMEM((RING, ZF, width), BF),
                pltpu.VMEM((RING, ZF, width), BF),
                pltpu.VMEM((RING, ZF, width), BF),
                pltpu.VMEM((5, 8, width), F32),
                pltpu.SemaphoreType.DMA((7,)),
                pltpu.SemaphoreType.DMA((4, 3)),
                pltpu.SemaphoreType.DMA((4, 3)),
                pltpu.SemaphoreType.DMA((4, 3)),
                pltpu.SemaphoreType.DMA((4, 3)),
                pltpu.SemaphoreType.DMA((KINDS, RING)),
                pltpu.SemaphoreType.DMA((KINDS, RING)),
                pltpu.SemaphoreType.DMA((RING,)),
                pltpu.SemaphoreType.DMA((5,)),
                pltpu.SemaphoreType.DMA((5,)),
            ],
            compiler_params=pltpu.CompilerParams(
                collective_id=0, has_side_effects=True, vmem_limit_bytes=HIGH
            ),
        )(lengths, tokens, cotangent, vecs, w_in, weight_out, weight_up, weight_down)
        g_down = gout[:f_cols].astype(F32)
        g_up = gout[f_cols : f_cols + width].astype(F32)
        g_in = gout[f_cols + width : f_cols + width + 3 * cols]
        g_in = g_in.reshape(heads, 3, HD, width).transpose(3, 1, 0, 2).reshape(width, 3, cols).astype(F32)
        g_out = gout[f_cols + width + 3 * cols :].astype(F32)
        gb_in = small[7, : 3 * cols].reshape(heads, 3, HD).transpose(1, 0, 2).reshape(3, cols)
        gb_in = jnp.stack([gb_in[0], gb_in[2]])
        return (lo, gtok, small[0], small[1], g_in, gb_in, g_out, small[2], small[3], small[4], g_up, small[6], g_down, small[5])

    rows2 = P(("dp", "tensor"), None)
    every = P()
    return jax.shard_map(
        local,
        mesh=mesh,
        in_specs=(rows2, P("dp"), every, every, P(None, None, "tensor"), P(None, "tensor"), P("tensor", None), every,
                  every, every, P(None, "tensor"), P("tensor"), P("tensor", None), every, rows2),
        out_specs=(rows2, rows2, every, every, P(None, None, "tensor"), P(None, "tensor"), P("tensor", None), every,
                   every, every, P(None, "tensor"), P("tensor"), P("tensor", None), every),
        check_vma=False,
    )
```

```python
import functools

import jax
import jax.numpy as jnp
from jax import lax
from jax.experimental import pallas as pl
from jax.experimental.pallas import tpu as pltpu
from jax.sharding import PartitionSpec as P

HD = 64
LEN = 1024
BF = jnp.bfloat16
F32 = jnp.float32
MESH = pl.DeviceIdType.MESH
LOG2E = 1.4426950408889634
LN2 = 0.6931471805599453
UNIT = 128
YH = UNIT // 4
YF = UNIT // 8
ZF = UNIT // 4
ZA0 = UNIT // 2
ZB0 = ZA0 + ZF
KINDS = 11
HIGH = 62 * 2**20


def dot(left, right, left_dim, right_dim):
    return lax.dot_general(
        left, right, (((left_dim,), (right_dim,)), ((), ())), preferred_element_type=F32
    )


def norm_parts(rows):
    centre = rows - jnp.mean(rows, axis=-1, keepdims=True)
    scale = lax.rsqrt(jnp.mean(centre * centre, axis=-1, keepdims=True) + 1e-05)
    return centre * scale, scale


def kernel(n_dp, len_ref, tok, cot, gain_1, shift_1, b_out, gain_2, shift_2, b_down, b_up, b_in, win_h, wout_h, wup_h, wdown_h,
           lo, gtok, small, gout, first_h,
           win, wout, wup, wdown, first, cotg, sec, act, gh,
           qkv, vt, kt, ctxT, dO, dk, dv, mid, gmid, bias, lse,
           ps, rcv, part, yR, zYA, zYB, zZA, zZB, yZ, smr,
           wsem, ag_s, ag_r, rs_s, rs_r, dp_s, dp_r, out_s, sm_s, sm_r):
    line = n_dp // 2
    width = tok.shape[1]
    rows = tok.shape[0]
    heads = dO.shape[0]
    units = gout.shape[0] // UNIT
    ring = part.shape[0] // UNIT
    gap = max(0, 2 * line + 2 - ring)
    starts = units + gap * ((units - 1) // ring)
    last = starts + 2 * line + 2
    small_at = last - 2 * line - 2
    branch = first
    first2 = act
    dmx = sec

    g = lax.axis_index("dp")
    t = lax.axis_index("tensor")
    cp = t + 1 - 2 * lax.rem(t, 2)
    xp = lax.rem(t + 2, 4)
    dg = lax.rem(cp + 2, 4)
    y = lax.rem(g, 2)
    zl = lax.div(g, 2)
    chip = lax.div(t, 2)
    core_dev = (g, cp)
    x_dev = (g, xp)
    y_dev = (g + 1 - 2 * y, t)
    up_dev = (g + 2, t)
    dn_dev = (g - 2, t)
    has_up = zl < line - 1
    has_dn = zl > 0

    def blk(b):
        return pl.ds(pl.multiple_of(b * rows, rows), rows)

    def rcopy(src, dst, s_sem, r_sem, dev):
        return pltpu.make_async_remote_copy(
            src_ref=src, dst_ref=dst, send_sem=s_sem, recv_sem=r_sem, device_id=dev, device_id_type=MESH
        )

    loads = [
        pltpu.make_async_copy(win_h, win, wsem.at[0]),
        pltpu.make_async_copy(wout_h, wout, wsem.at[1]),
        pltpu.make_async_copy(wup_h, wup, wsem.at[2]),
        pltpu.make_async_copy(wdown_h, wdown, wsem.at[3]),
    ]
    for item in loads:
        item.start()

    barrier = pltpu.get_barrier_semaphore()
    for dev in (core_dev, x_dev, y_dev):
        pl.semaphore_signal(barrier, inc=1, device_id=dev, device_id_type=MESH)

    @pl.when(has_up)
    def _():
        pl.semaphore_signal(barrier, inc=1, device_id=up_dev, device_id_type=MESH)

    @pl.when(has_dn)
    def _():
        pl.semaphore_signal(barrier, inc=1, device_id=dn_dev, device_id_type=MESH)

    class Gather:
        def __init__(self, buf, at):
            own, theirs = buf.at[blk(t), :], buf.at[blk(xp), :]
            self.x = rcopy(own, own, ag_s.at[at, 0], ag_r.at[at, 0], x_dev)
            self.c = rcopy(own, own, ag_s.at[at, 1], ag_r.at[at, 1], core_dev)
            self.f = rcopy(theirs, theirs, ag_s.at[at, 2], ag_r.at[at, 2], core_dev)

        def start(self):
            self.x.start()
            self.c.start()

        def drain(self):
            self.x.wait_send()
            self.c.wait_send()
            self.f.wait_send()

        def near(self):
            self.c.wait_recv()

        def far(self):
            self.x.wait_recv()
            self.f.start()

        def diag(self):
            self.f.wait_recv()

    class Scatter:
        def __init__(self, at, slot):
            self.own_in, self.x_relay, self.x_in = (rcv.at[slot, i] for i in range(3))
            self.d = rcopy(ps.at[0], rcv.at[slot, 1], rs_s.at[at, 0], rs_r.at[at, 0], core_dev)
            self.x = rcopy(ps.at[1], rcv.at[slot, 2], rs_s.at[at, 1], rs_r.at[at, 1], x_dev)
            self.c = rcopy(ps.at[2], rcv.at[slot, 0], rs_s.at[at, 2], rs_r.at[at, 2], core_dev)

        def far(self, fn, send=True):
            fn(dg, functools.partial(self.put, 0))
            self.d.start()
            fn(xp, functools.partial(self.put, 1))
            self.d.wait_recv()

            def add(i, _):
                r = pl.ds(pl.multiple_of(i * 64, 64), 64)
                ps[1, r, :] = (ps[1, r, :].astype(F32) + self.x_relay[r, :].astype(F32)).astype(BF)
                return 0

            lax.fori_loop(0, rows // 64, add, 0)
            if send:
                self.x.start()

        @staticmethod
        def put(slot, cols, value):
            ps[slot, :, cols] = value.astype(BF)

        def close(self, fn, total):
            fn(cp, functools.partial(self.put, 2))
            self.c.start()

            def keep(cols, value):
                total[:, cols] = value

            fn(t, keep)

        def wait(self):
            self.c.wait_recv()
            self.x.wait_recv()

        def extra(self, r):
            return self.own_in[r, :].astype(F32) + self.x_in[r, :].astype(F32)

        def drain(self):
            self.d.wait_send()
            self.x.wait_send()
            self.c.wait_send()

    def unit_of(m):
        if gap == 0:
            return (m >= 0) & (m < units), m
        late = m >= ring + gap
        u = jnp.where(late, m - gap, m)
        return (m >= 0) & (u < units) & (late | (m < ring)), u

    R_OWN, R_OTHER = (y * YH, YH), ((1 - y) * YH, YH)
    R_YA, R_YB = (y * YH, YF), (y * YH + YF, YF)
    R_ZA, R_ZB = (ZA0, ZF), (ZB0, ZF)

    def at(s, where):
        start, count = where
        return pl.ds(pl.multiple_of(s * UNIT + start, count), count)

    def dcopy(kind, s, src_rows, dst, dev):
        return rcopy(part.at[at(s, src_rows), :], dst, dp_s.at[kind, s], dp_r.at[kind, s], dev)

    def c_y(s):
        return dcopy(0, s, R_OTHER, yR.at[s], y_dev)

    def c_ya(s):
        return dcopy(1, s, R_YA, zYA.at[s], dn_dev)

    def c_yb(s):
        return dcopy(2, s, R_YB, zYB.at[s], up_dev)

    def c_za(s):
        return dcopy(3, s, R_ZA, zZA.at[s], dn_dev)

    def c_zb(s):
        return dcopy(4, s, R_ZB, zZB.at[s], up_dev)

    def c_ex(s, which):
        return dcopy(5, s, which, yZ.at[s], y_dev)

    def b_ya(s):
        return dcopy(6, s, R_YA, zYA.at[s], up_dev)

    def b_yb(s):
        return dcopy(7, s, R_YB, zYB.at[s], dn_dev)

    def b_y(s):
        return dcopy(8, s, R_OWN, part.at[at(s, R_OWN), :], y_dev)

    def b_za(s):
        return dcopy(9, s, R_ZA, zZA.at[s], up_dev)

    def b_zb(s):
        return dcopy(10, s, R_ZB, zZB.at[s], dn_dev)

    def add_in(s, where, got):
        r = at(s, where)
        part[r, :] = (part[r, :].astype(F32) + got[s].astype(F32)).astype(BF)

    def out_copy(s, u):
        return pltpu.make_async_copy(
            part.at[at(s, (0, UNIT)), :], gout.at[pl.ds(pl.multiple_of(u * UNIT, UNIT), UNIT), :], out_s.at[s]
        )

    def on(m, cond, fn):
        ok, u = unit_of(m)
        if cond is not None:
            ok = ok & cond

        @pl.when(ok)
        def _():
            fn(lax.rem(u, ring), u)

    def step(n):
        def begin(s, u):
            c_y(s).start()

            @pl.when(zl == line - 1)
            def _():
                c_za(s).start()

            @pl.when(zl == 0)
            def _():
                c_zb(s).start()

        def pair_sum(s, u):
            c_y(s).wait()
            add_in(s, R_OWN, yR)

            @pl.when(zl == line - 1)
            def _():
                c_ya(s).start()

            @pl.when(zl == 0)
            def _():
                c_yb(s).start()

        def line_zb(s, u):
            c_zb(s).wait_recv()
            add_in(s, R_ZB, zZB)

            @pl.when(has_up)
            def _():
                c_zb(s).start()

            @pl.when(zl == line - 1)
            def _():
                c_ex(s, R_ZB).start()

        def line_za(s, u):
            c_za(s).wait_recv()
            add_in(s, R_ZA, zZA)

            @pl.when(has_dn)
            def _():
                c_za(s).start()

            @pl.when(zl == 0)
            def _():
                c_ex(s, R_ZA).start()

        def pair_za(s, u):
            c_ex(s, R_ZA).wait()
            add_in(s, R_ZA, yZ)
            b_za(s).start()

        def pair_zb(s, u):
            c_ex(s, R_ZB).wait()
            add_in(s, R_ZB, yZ)
            b_zb(s).start()

        def line_yb(s, u):
            c_yb(s).wait_recv()
            add_in(s, R_YB, zYB)

            @pl.when(has_up)
            def _():
                c_yb(s).start()

            @pl.when(zl == line - 1)
            def _():
                b_yb(s).start()

        def line_ya(s, u):
            c_ya(s).wait_recv()
            add_in(s, R_YA, zYA)

            @pl.when(has_dn)
            def _():
                c_ya(s).start()

            @pl.when(zl == 0)
            def _():
                b_ya(s).start()

        def back_a(s, u):
            c_za(s).wait_send()
            c_ya(s).wait_send()
            b_za(s).wait_recv()
            b_ya(s).wait_recv()
            part[at(s, R_ZA), :] = zZA[s]
            part[at(s, R_YA), :] = zYA[s]

            @pl.when(has_up)
            def _():
                b_za(s).start()
                b_ya(s).start()

        def back_b(s, u):
            c_zb(s).wait_send()
            c_yb(s).wait_send()
            b_zb(s).wait_recv()
            b_yb(s).wait_recv()
            part[at(s, R_ZB), :] = zZB[s]
            part[at(s, R_YB), :] = zYB[s]

            @pl.when(has_dn)
            def _():
                b_zb(s).start()
                b_yb(s).start()

        def back_pair(s, u):
            b_y(s).start()

        def finish(s, u):
            b_y(s).wait_recv()
            out_copy(s, u).start()

        def drain(s, u):
            out_copy(s, u).wait()
            b_y(s).wait_send()

            @pl.when(has_up)
            def _():
                for item in (b_ya, b_za):
                    item(s).wait_send()

            @pl.when(has_dn)
            def _():
                for item in (b_yb, b_zb):
                    item(s).wait_send()

        on(n, None, begin)
        on(n - 1, None, pair_sum)
        on(n - zl, has_dn, line_zb)
        on(n - (line - 1 - zl), has_up, line_za)
        on(n - line, zl == 0, pair_za)
        on(n - line, zl == line - 1, pair_zb)
        on(n - 1 - zl, has_dn, line_yb)
        on(n - line + zl, has_up, line_ya)
        on(n - line - zl, has_dn, back_a)
        on(n - line - (line - 1 - zl), has_up, back_b)
        on(n - 2 * line + 1, None, back_pair)
        on(n - 2 * line, None, finish)
        on(n - 2 * line - 1, None, drain)

    shared = lax.broadcasted_iota(jnp.int32, (8, width), 0) < 6

    def s_copy(i, src, dst, dev):
        return rcopy(src, dst, sm_s.at[i], sm_r.at[i], dev)

    def small_step(n):
        core = s_copy(0, small, smr.at[0], core_dev)
        across = s_copy(1, small, smr.at[1], x_dev)
        pair = s_copy(2, small, smr.at[2], y_dev)
        down = s_copy(3, small, smr.at[3], dn_dev)
        back = s_copy(4, small, smr.at[4], up_dev)

        def when(m, cond, fn):
            ok = n == small_at + m
            if cond is not None:
                ok = ok & cond
            pl.when(ok)(fn)

        def s0():
            core.start()

        def s1():
            core.wait()
            small[...] = small[...] + jnp.where(shared, smr[0], 0.0)
            across.start()

        def s2():
            across.wait()
            small[...] = small[...] + jnp.where(shared, smr[1], 0.0)
            pair.start()

        def s3():
            pair.wait()
            small[...] = small[...] + smr[2]

            @pl.when(zl == line - 1)
            def _():
                down.start()

        def s4():
            down.wait_recv()
            small[...] = small[...] + smr[3]

            @pl.when(has_dn)
            def _():
                down.start()

            @pl.when(zl == 0)
            def _():
                back.start()

        def s5():
            back.wait_recv()

            @pl.when(has_dn & (zl > 0))
            def _():
                down.wait_send()

            small[...] = smr[4]

            @pl.when(has_up)
            def _():
                back.start()

        when(0, None, s0)
        when(1, None, s1)
        when(2, None, s2)
        when(3, None, s3)
        when(3 + line - 1 - zl, has_up, s4)
        when(3 + line - 1 + zl, has_dn, s5)

    def steps(lo_n, hi_n):
        def body(n, _):
            step(n)
            small_step(n)
            return 0

        lax.fori_loop(lo_n, hi_n, body, 0)

    keys = lax.broadcasted_iota(jnp.int32, (LEN, 128), 0)
    bias[...] = jnp.where(keys < len_ref[0], 0.0, -1e30)
    gain_one, shift_one = gain_1[...].reshape(1, width), shift_1[...].reshape(1, width)
    gain_two, shift_two = gain_2[...].reshape(1, width), shift_2[...].reshape(1, width)
    bias_out, bias_down = b_out[...].reshape(1, width), b_down[...].reshape(1, width)
    CH = 32

    def norm_one(i, _):
        r = pl.ds(pl.multiple_of(i * CH, CH), CH)
        n, _s = norm_parts(tok[r, :].astype(F32))
        first[pl.ds(pl.multiple_of(t * rows + i * CH, CH), CH), :] = (n * gain_one + shift_one).astype(BF)
        return 0

    lax.fori_loop(0, rows // CH, norm_one, 0)
    pl.semaphore_wait(barrier, 3 + has_up.astype(jnp.int32) + has_dn.astype(jnp.int32))
    gather_first = Gather(first, 0)
    gather_first.start()
    own_cot = pltpu.make_async_copy(cot, cotg.at[blk(t), :], wsem.at[4])
    own_cot.start()
    loads[0].wait()

    cols_qkv = 3 * heads * HD

    def project(b):
        f = first[blk(b), :]
        for base in range(0, cols_qkv, 384):
            w = min(384, cols_qkv - base)
            mixed = dot(f, win[base : base + w, :], 1, 1)
            for i in range(base // HD, (base + w) // HD):
                which, h = i // heads, i % heads
                piece = mixed[:, i * HD - base : (i + 1) * HD - base]
                if which != 1:
                    row = which // 2
                    piece = piece + b_in[row : row + 1, h * HD : (h + 1) * HD]
                piece = piece.astype(BF)
                qkv[i, blk(b), :] = piece
                if which == 1:
                    kt[h, :, blk(b)] = piece.T
                if which == 2:
                    vt[h, :, blk(b)] = piece.T

    project(t)
    gather_first.near()
    project(cp)
    gather_first.far()
    own_cot.wait()
    gather_cot = Gather(cotg, 1)
    gather_cot.start()
    project(xp)
    gather_first.diag()
    project(dg)
    keep_first = pltpu.make_async_copy(first, first_h, wsem.at[5])
    keep_first.start()

    HALF = 2 * rows
    SCALE = HD**-0.5

    def half(i):
        return pl.ds(pl.multiple_of(i * HALF, HALF), HALF)

    def attend(i):
        def head(h, _):
            q = qkv[h, half(i), :]
            k = qkv[heads + h]
            s = dot(k, q, 1, 1) * (SCALE * LOG2E) + bias[:, 0:1]
            top = jnp.max(s, axis=0, keepdims=True)
            p = jnp.exp2(s - top)
            total = jnp.sum(p, axis=0, keepdims=True)
            o = dot(vt[h], p.astype(BF), 1, 0) / total
            ctxT[pl.ds(pl.multiple_of(h * HD, HD), HD), half(i)] = o.astype(BF)
            lse[h, i] = top + jnp.log2(total)
            return 0

        lax.fori_loop(0, heads, head, 0)

    def tiles(n_cols, fn):
        for c0 in range(0, n_cols, 256):
            fn(slice(c0, c0 + 256))

    def project_out(b, put):
        left = ctxT[:, blk(b)]
        tiles(width, lambda c: put(c, dot(left, wout[:, c], 0, 0)))

    loads[1].wait()
    attend(1 - chip)
    sum_out = Scatter(0, 0)
    sum_out.far(project_out)
    attend(chip)
    gather_cot.near()
    gather_cot.far()
    sum_out.close(project_out, mid)
    sum_out.wait()

    def norm_two(i, _):
        r = pl.ds(pl.multiple_of(i * CH, CH), CH)
        v = tok[r, :].astype(F32) + (mid[r, :] + sum_out.extra(r) + bias_out)
        mid[r, :] = v
        n, _s = norm_parts(v)
        sec[pl.ds(pl.multiple_of(t * rows + i * CH, CH), CH), :] = (n * gain_two + shift_two).astype(BF)
        return 0

    lax.fori_loop(0, rows // CH, norm_two, 0)
    keep_first.wait()
    gather_first.drain()
    gather_sec = Gather(sec, 2)
    gather_sec.start()
    sum_out.drain()
    gather_cot.diag()
    loads[2].wait()
    loads[3].wait()

    small[...] = jnp.zeros((8, width), F32)
    f_cols = wup.shape[1]

    def feed_cols(b, c):
        hid = dot(sec[blk(b), :], wup[:, c], 1, 0) + b_up[c].reshape(1, 256)
        phi = 0.5 * (1.0 + lax.erf(hid * 0.7071067811865476))
        act[blk(b), c] = (hid * phi).astype(BF)
        slope = phi + hid * (0.3989422804014327 * jnp.exp(hid * hid * -0.5))
        grad = (dot(cotg[blk(b), :], wdown[c, :], 1, 1) * slope).astype(BF)
        gh[blk(b), c] = grad
        small[6:7, c] = small[6:7, c] + jnp.sum(grad.astype(F32), axis=0, keepdims=True)

    def chunk(i):
        return pl.ds(pl.multiple_of(i * 256, 256), 256)

    def feed(b):
        def cols(i, _):
            feed_cols(b, chunk(i))
            return 0

        lax.fori_loop(0, f_cols // 256, cols, 0)

    def weight_rows(base, left, c, right):
        lhs = left[:, c]
        r = pl.ds(pl.multiple_of(base, 64), lhs.shape[1])
        tiles(width, lambda cc: part.__setitem__((r, cc), dot(lhs, right[:, cc], 0, 0).astype(BF)))

    feed(t)
    gather_sec.near()
    feed(cp)
    gather_sec.far()
    gather_sec.diag()

    n_feed = f_cols // 256
    n_up = width // 256

    def feed_far(i, _):
        feed_cols(xp, chunk(i))
        feed_cols(dg, chunk(i))
        weight_rows(i * 256, act, chunk(i), cotg)
        step(i)
        return 0

    lax.fori_loop(0, n_feed, feed_far, 0)

    def back_up(b, put):
        left = gh[blk(b), :]
        tiles(width, lambda c: put(c, dot(left, wup[c, :], 1, 1)))

    sum_sec = Scatter(1, 1)
    sum_sec.far(back_up)
    sum_sec.close(back_up, gmid)

    def up_rows(i, _):
        weight_rows(f_cols + i * 256, sec, chunk(i), gh)
        step(n_feed + i)
        return 0

    lax.fori_loop(0, n_up, up_rows, 0)
    sum_sec.wait()
    now = n_feed + n_up

    zero_rows = jnp.zeros((1, width), F32)

    def total(v):
        return jnp.sum(v, axis=0, keepdims=True)

    def middle_back(i, carry):
        d_gain, d_shift, d_out, d_down = carry
        r = pl.ds(pl.multiple_of(i * CH, CH), CH)
        e = gmid[r, :] + sum_sec.extra(r)
        n, scale = norm_parts(mid[r, :])
        tt = e * gain_two
        inner = (tt - jnp.mean(tt, -1, keepdims=True) - n * jnp.mean(tt * n, -1, keepdims=True)) * scale
        c_rows = cot[r, :].astype(F32)
        gm = c_rows + inner
        gmid[r, :] = gm
        low = gm.astype(BF)
        branch[pl.ds(pl.multiple_of(t * rows + i * CH, CH), CH), :] = low
        return (
            d_gain + total(e * n), d_shift + total(e), d_out + total(low.astype(F32)), d_down + total(c_rows)
        )

    d_gain, d_shift, d_out, d_down = lax.fori_loop(0, rows // CH, middle_back, (zero_rows,) * 4)
    small[3:4, :] = d_gain
    small[4:5, :] = d_shift
    small[2:3, :] = d_out
    small[5:6, :] = d_down
    gather_branch = Gather(branch, 3)
    gather_branch.start()
    sum_sec.drain()
    step(now)

    def down(b, put):
        left = act[blk(b), :]
        tiles(width, lambda c: put(c, dot(left, wdown[:, c], 1, 0)))

    sum_down = Scatter(2, 0)
    sum_down.far(down, send=False)
    step(now + 1)
    sum_down.close(down, lo)
    load_first = pltpu.make_async_copy(first_h, first2, wsem.at[6])
    load_first.start()
    step(now + 2)
    now = now + 3

    def back_out(b):
        grad = dot(branch[blk(b), :], wout[...], 1, 1).astype(BF)
        for h in range(heads):
            dO[h, blk(b), :] = grad[:, h * HD : (h + 1) * HD]

    back_out(t)
    gather_branch.near()
    back_out(cp)
    gather_branch.far()
    sum_down.x.start()
    back_out(xp)
    gather_branch.diag()
    back_out(dg)

    def attend_back(h, _):
        k = qkv[heads + h]
        v = qkv[2 * heads + h]
        for i in range(LEN // HALF):
            r = slice(i * HALF, (i + 1) * HALF)
            q = qkv[h, r, :]
            o_grad = dO[h, r, :]
            s = dot(k, q, 1, 1) * (SCALE * LOG2E) + bias[:, 0:1]
            p = jnp.exp2(s - lse[h, i])
            dp = dot(v, o_grad, 1, 1)
            delta = jnp.sum(p * dp, axis=0, keepdims=True)
            ds = (p * (dp - delta)).astype(BF)
            d_v = dot(p.astype(BF), o_grad, 1, 0)
            d_k = dot(ds, q, 1, 0)
            if i == 0:
                dv[...] = d_v
                dk[...] = d_k
            else:
                dv[...] = dv[...] + d_v
                dk[...] = dk[...] + d_k
            d_q = dot(kt[h], ds, 1, 0) * SCALE
            qkv[h, r, :] = d_q.T.astype(BF)
        qkv[heads + h] = (dk[...] * SCALE).astype(BF)
        qkv[2 * heads + h] = dv[...].astype(BF)
        step(now + h)
        return 0

    lax.fori_loop(0, heads, attend_back, 0)
    now = now + heads
    assert now <= ring

    def assemble(i, carry):
        r = pl.ds(pl.multiple_of(i * 256, 256), 256)
        for p in range(3 * heads):
            dmx[r, p * HD : (p + 1) * HD] = qkv[p, r, :]
        return carry + total(dmx[r, 0:cols_qkv].astype(F32))

    gather_sec.drain()
    small[7:8, 0:cols_qkv] = lax.fori_loop(0, LEN // 256, assemble, jnp.zeros((1, cols_qkv), F32))

    def back_first(b, put):
        left = dmx[blk(b), 0:cols_qkv]
        tiles(width, lambda c: put(c, dot(left, win[:, c], 1, 0)))

    sum_down.drain()
    sum_first = Scatter(3, 1)
    sum_first.far(back_first)
    sum_first.close(back_first, gtok)
    load_first.wait()

    steps(now, ring + gap)
    now = ring + gap
    for base in range(0, cols_qkv, 256):
        weight_rows(base, dmx, slice(base, min(base + 256, cols_qkv)), first2)
    tiles(width, lambda c: part.__setitem__(
        (slice(cols_qkv, cols_qkv + heads * HD), c), dot(ctxT[...], branch[:, c], 1, 0).astype(BF)))
    step(now)
    sum_down.wait()

    def finish_out(i, _):
        r = pl.ds(pl.multiple_of(i * CH, CH), CH)
        lo[r, :] = mid[r, :] + lo[r, :] + sum_down.extra(r) + bias_down
        return 0

    lax.fori_loop(0, rows // CH, finish_out, 0)
    step(now + 1)
    sum_first.wait()

    def tokens_back(i, carry):
        d_gain, d_shift = carry
        r = pl.ds(pl.multiple_of(i * CH, CH), CH)
        e = gtok[r, :] + sum_first.extra(r)
        n, scale = norm_parts(tok[r, :].astype(F32))
        tt = e * gain_one
        inner = (tt - jnp.mean(tt, -1, keepdims=True) - n * jnp.mean(tt * n, -1, keepdims=True)) * scale
        gtok[r, :] = gmid[r, :] + inner
        return (d_gain + total(e * n), d_shift + total(e))

    d_gain, d_shift = lax.fori_loop(0, rows // CH, tokens_back, (zero_rows,) * 2)
    small[0:1, :] = d_gain
    small[1:2, :] = d_shift
    steps(now + 2, last)

    gather_cot.drain()
    gather_branch.drain()
    sum_first.drain()

    @pl.when(has_up)
    def _():
        s_copy(4, small, smr.at[4], up_dev).wait_send()


def solution(mesh):
    n_dp = mesh.shape["dp"]

    def local(tokens, lengths, gain_one, shift_one, weight_in, bias_in, weight_out, bias_out, gain_two, shift_two,
              weight_up, bias_up, weight_down, bias_down, cotangent):
        rows, width = tokens.shape
        cols = weight_in.shape[2]
        heads = cols // HD
        f_cols = weight_up.shape[1]
        w_in = weight_in.transpose(1, 2, 0).reshape(3 * cols, width)
        total = 4 * rows
        g_rows = f_cols + width + 4 * cols
        ring = (f_cols + width) // UNIT
        vm = pl.BlockSpec(memory_space=pltpu.VMEM)
        hb = pl.BlockSpec(memory_space=pl.ANY)
        big = pltpu.VMEM((total, width), BF)
        lo, gtok, small, gout, _first = pl.pallas_call(
            functools.partial(kernel, n_dp),
            out_shape=[
                jax.ShapeDtypeStruct((rows, width), F32),
                jax.ShapeDtypeStruct((rows, width), F32),
                jax.ShapeDtypeStruct((8, width), F32),
                jax.ShapeDtypeStruct((g_rows, width), BF),
                jax.ShapeDtypeStruct((total, width), BF),
            ],
            in_specs=[pl.BlockSpec(memory_space=pltpu.SMEM)] + [vm] * 10 + [hb] * 4,
            out_specs=[vm, vm, vm, hb, hb],
            scratch_shapes=[
                pltpu.VMEM((3 * cols, width), BF),
                pltpu.VMEM((cols, width), BF),
                pltpu.VMEM((width, f_cols), BF),
                pltpu.VMEM((f_cols, width), BF),
                big, big, big,
                pltpu.VMEM((total, f_cols), BF),
                pltpu.VMEM((total, f_cols), BF),
                pltpu.VMEM((3 * heads, LEN, HD), BF),
                pltpu.VMEM((heads, HD, LEN), BF),
                pltpu.VMEM((heads, HD, LEN), BF),
                pltpu.VMEM((cols, LEN), BF),
                pltpu.VMEM((heads, LEN, HD), BF),
                pltpu.VMEM((LEN, HD), F32),
                pltpu.VMEM((LEN, HD), F32),
                pltpu.VMEM((rows, width), F32),
                pltpu.VMEM((rows, width), F32),
                pltpu.VMEM((LEN, 128), F32),
                pltpu.VMEM((heads, 2, 1, 2 * rows), F32),
                pltpu.VMEM((3, rows, width), BF),
                pltpu.VMEM((2, 3, rows, width), BF),
                pltpu.VMEM((ring * UNIT, width), BF),
                pltpu.VMEM((ring, YH, width), BF),
                pltpu.VMEM((ring, YF, width), BF),
                pltpu.VMEM((ring, YF, width), BF),
                pltpu.VMEM((ring, ZF, width), BF),
                pltpu.VMEM((ring, ZF, width), BF),
                pltpu.VMEM((ring, ZF, width), BF),
                pltpu.VMEM((5, 8, width), F32),
                pltpu.SemaphoreType.DMA((7,)),
                pltpu.SemaphoreType.DMA((4, 3)),
                pltpu.SemaphoreType.DMA((4, 3)),
                pltpu.SemaphoreType.DMA((4, 3)),
                pltpu.SemaphoreType.DMA((4, 3)),
                pltpu.SemaphoreType.DMA((KINDS, ring)),
                pltpu.SemaphoreType.DMA((KINDS, ring)),
                pltpu.SemaphoreType.DMA((ring,)),
                pltpu.SemaphoreType.DMA((5,)),
                pltpu.SemaphoreType.DMA((5,)),
            ],
            compiler_params=pltpu.CompilerParams(
                collective_id=0, has_side_effects=True, vmem_limit_bytes=HIGH
            ),
        )(lengths, tokens, cotangent, gain_one, shift_one, bias_out, gain_two, shift_two, bias_down, bias_up, bias_in,
          w_in, weight_out, weight_up, weight_down)
        g_down = gout[:f_cols].astype(F32)
        g_up = gout[f_cols : f_cols + width].astype(F32)
        g_in = gout[f_cols + width : f_cols + width + 3 * cols]
        g_in = g_in.astype(F32).reshape(3, cols, width).transpose(2, 0, 1)
        g_out = gout[f_cols + width + 3 * cols :].astype(F32)
        gb_in = small[7, : 3 * cols].reshape(3, cols)
        gb_in = jnp.stack([gb_in[0], gb_in[2]])
        return (lo, gtok, small[0], small[1], g_in, gb_in, g_out, small[2], small[3], small[4], g_up, small[6], g_down, small[5])

    rows2 = P(("dp", "tensor"), None)
    every = P()
    return jax.shard_map(
        local,
        mesh=mesh,
        in_specs=(rows2, P("dp"), every, every, P(None, None, "tensor"), P(None, "tensor"), P("tensor", None), every,
                  every, every, P(None, "tensor"), P("tensor"), P("tensor", None), every, rows2),
        out_specs=(rows2, rows2, every, every, P(None, None, "tensor"), P(None, "tensor"), P("tensor", None), every,
                   every, every, P(None, "tensor"), P("tensor"), P("tensor", None), every),
        check_vma=False,
    )
```

```python
import functools

import jax
import jax.numpy as jnp
from jax import lax
from jax.experimental import pallas as pl
from jax.experimental.pallas import tpu as pltpu
from jax.sharding import PartitionSpec as P

HD = 64
LEN = 1024
BF = jnp.bfloat16
F32 = jnp.float32
MESH = pl.DeviceIdType.MESH
LOG2E = 1.4426950408889634
LN2 = 0.6931471805599453
UNIT = 128
YH = UNIT // 4
YF = UNIT // 8
ZF = UNIT // 4
ZA0 = UNIT // 2
ZB0 = ZA0 + ZF
KINDS = 11
SLOTS = 10
HIGH = 62 * 2**20


def dot(left, right, left_dim, right_dim):
    return lax.dot_general(
        left, right, (((left_dim,), (right_dim,)), ((), ())), preferred_element_type=F32
    )


def norm_parts(rows):
    centre = rows - jnp.mean(rows, axis=-1, keepdims=True)
    scale = lax.rsqrt(jnp.mean(centre * centre, axis=-1, keepdims=True) + 1e-05)
    return centre * scale, scale


def kernel(n_dp, len_ref, tok, cot, gain_1, shift_1, b_out, gain_2, shift_2, b_down, b_up, b_in, win_h, wout_h, wup_h, wdown_h,
           lo_h, gtok_h, small, gout, first_h,
           lo, gtok, win, wout, wup, wdown, first, cotg, sec, act, gh,
           qkv, vt, kt, ctxT, dO, dk, dv, mid, gmid, bias, lse,
           ps, rcv, part, yR, zYA, zYB, zZA, zZB, yZ, smr,
           wsem, ag_s, ag_r, rs_s, rs_r, dp_s, dp_r, out_s, sm_s, sm_r):
    line = n_dp // 2
    width = tok.shape[1]
    rows = tok.shape[0]
    heads = dO.shape[0]
    units = gout.shape[0] // UNIT
    ring = part.shape[0] // UNIT
    gap = max(0, 2 * line + 2 - SLOTS)

    def start_of(u):
        return u + gap * (u // SLOTS)

    small_at = start_of(units - 1)
    last = small_at + 2 * line + 2
    branch = first
    first2 = act
    dmx = sec

    g = lax.axis_index("dp")
    t = lax.axis_index("tensor")
    cp = t + 1 - 2 * lax.rem(t, 2)
    xp = lax.rem(t + 2, 4)
    dg = lax.rem(cp + 2, 4)
    y = lax.rem(g, 2)
    zl = lax.div(g, 2)
    chip = lax.div(t, 2)
    core_dev = (g, cp)
    x_dev = (g, xp)
    y_dev = (g + 1 - 2 * y, t)
    up_dev = (g + 2, t)
    dn_dev = (g - 2, t)
    has_up = zl < line - 1
    has_dn = zl > 0

    def blk(b):
        return pl.ds(pl.multiple_of(b * rows, rows), rows)

    def rcopy(src, dst, s_sem, r_sem, dev):
        return pltpu.make_async_remote_copy(
            src_ref=src, dst_ref=dst, send_sem=s_sem, recv_sem=r_sem, device_id=dev, device_id_type=MESH
        )

    loads = [
        pltpu.make_async_copy(win_h, win, wsem.at[0]),
        pltpu.make_async_copy(wout_h, wout, wsem.at[1]),
        pltpu.make_async_copy(wup_h, wup, wsem.at[2]),
        pltpu.make_async_copy(wdown_h, wdown, wsem.at[3]),
    ]
    for item in loads:
        item.start()

    barrier = pltpu.get_barrier_semaphore()
    for dev in (core_dev, x_dev, y_dev):
        pl.semaphore_signal(barrier, inc=1, device_id=dev, device_id_type=MESH)

    @pl.when(has_up)
    def _():
        pl.semaphore_signal(barrier, inc=1, device_id=up_dev, device_id_type=MESH)

    @pl.when(has_dn)
    def _():
        pl.semaphore_signal(barrier, inc=1, device_id=dn_dev, device_id_type=MESH)

    hrows = rows // 2

    def piece_rows(b, i):
        return pl.ds(pl.multiple_of(b * rows + i * hrows, hrows), hrows)

    class Gather:
        def __init__(self, buf, at):
            own = buf.at[blk(t), :]
            self.c = rcopy(own, own, ag_s.at[at, 4], ag_r.at[at, 4], core_dev)
            self.x, self.f = [], []
            for i in range(2):
                mine, theirs = buf.at[piece_rows(t, i), :], buf.at[piece_rows(xp, i), :]
                self.x.append(rcopy(mine, mine, ag_s.at[at, i], ag_r.at[at, i], x_dev))
                self.f.append(rcopy(theirs, theirs, ag_s.at[at, 2 + i], ag_r.at[at, 2 + i], core_dev))

        def start(self):
            self.x[0].start()
            self.x[1].start()
            self.c.start()

        def drain(self):
            for item in self.x + [self.c] + self.f:
                item.wait_send()

        def near(self):
            self.c.wait_recv()

        def far(self):
            for i in range(2):
                self.x[i].wait_recv()
                self.f[i].start()

        def diag(self):
            self.f[0].wait_recv()
            self.f[1].wait_recv()

    class Scatter:
        def __init__(self, at, slot):
            self.own_in, self.x_relay, self.x_in = (rcv.at[slot, i] for i in range(3))
            self.d = rcopy(ps.at[0], rcv.at[slot, 1], rs_s.at[at, 0], rs_r.at[at, 0], core_dev)
            self.x = []
            for i in range(2):
                r = pl.ds(i * hrows, hrows)
                self.x.append(
                    rcopy(ps.at[1, r, :], rcv.at[slot, 2, r, :], rs_s.at[at, 2 + i], rs_r.at[at, 2 + i], x_dev)
                )
            self.c = rcopy(ps.at[2], rcv.at[slot, 0], rs_s.at[at, 1], rs_r.at[at, 1], core_dev)

        def far(self, fn, send=True):
            fn(dg, functools.partial(self.put, 0))
            self.d.start()
            fn(xp, functools.partial(self.put, 1))
            self.d.wait_recv()

            def add(i, _):
                r = pl.ds(pl.multiple_of(i * 64, 64), 64)
                ps[1, r, :] = (ps[1, r, :].astype(F32) + self.x_relay[r, :].astype(F32)).astype(BF)
                return 0

            lax.fori_loop(0, rows // 64, add, 0)
            if send:
                self.send()

        def send(self):
            self.x[0].start()
            self.x[1].start()

        @staticmethod
        def put(slot, cols, value):
            ps[slot, :, cols] = value.astype(BF)

        def close(self, fn, total):
            fn(cp, functools.partial(self.put, 2))
            self.c.start()

            def keep(cols, value):
                total[:, cols] = value

            fn(t, keep)

        def wait(self):
            self.c.wait_recv()
            self.x[0].wait_recv()
            self.x[1].wait_recv()

        def extra(self, r):
            return self.own_in[r, :].astype(F32) + self.x_in[r, :].astype(F32)

        def drain(self):
            for item in [self.d, self.c] + self.x:
                item.wait_send()

    def unit_of(m):
        if gap == 0:
            return (m >= 0) & (m < units), m
        r = lax.rem(m, SLOTS + gap)
        u = lax.div(m, SLOTS + gap) * SLOTS + r
        return (m >= 0) & (r < SLOTS) & (u < units), u

    R_OWN, R_OTHER = (y * YH, YH), ((1 - y) * YH, YH)
    R_YA, R_YB = (y * YH, YF), (y * YH + YF, YF)
    R_ZA, R_ZB = (ZA0, ZF), (ZB0, ZF)

    def at(s, where):
        start, count = where
        return pl.ds(pl.multiple_of(s[0] * UNIT + start, count), count)

    def dcopy(kind, s, src_rows, dst, dev):
        return rcopy(part.at[at(s, src_rows), :], dst, dp_s.at[kind, s[1]], dp_r.at[kind, s[1]], dev)

    def c_y(s):
        return dcopy(0, s, R_OTHER, yR.at[s[1]], y_dev)

    def c_ya(s):
        return dcopy(1, s, R_YA, zYA.at[s[1]], dn_dev)

    def c_yb(s):
        return dcopy(2, s, R_YB, zYB.at[s[1]], up_dev)

    def c_za(s):
        return dcopy(3, s, R_ZA, zZA.at[s[1]], dn_dev)

    def c_zb(s):
        return dcopy(4, s, R_ZB, zZB.at[s[1]], up_dev)

    def c_ex(s, which):
        return dcopy(5, s, which, yZ.at[s[1]], y_dev)

    def b_ya(s):
        return dcopy(6, s, R_YA, zYA.at[s[1]], up_dev)

    def b_yb(s):
        return dcopy(7, s, R_YB, zYB.at[s[1]], dn_dev)

    def b_y(s):
        return dcopy(8, s, R_OWN, part.at[at(s, R_OWN), :], y_dev)

    def b_za(s):
        return dcopy(9, s, R_ZA, zZA.at[s[1]], up_dev)

    def b_zb(s):
        return dcopy(10, s, R_ZB, zZB.at[s[1]], dn_dev)

    def add_in(s, where, got):
        r = at(s, where)
        part[r, :] = (part[r, :].astype(F32) + got[s[1]].astype(F32)).astype(BF)

    def out_copy(s, u):
        return pltpu.make_async_copy(
            part.at[at(s, (0, UNIT)), :], gout.at[pl.ds(pl.multiple_of(u * UNIT, UNIT), UNIT), :], out_s.at[s[1]]
        )

    def on(m, cond, fn):
        ok, u = unit_of(m)
        if cond is not None:
            ok = ok & cond

        @pl.when(ok)
        def _():
            fn((lax.rem(u, ring), lax.rem(u, SLOTS)), u)

    def step(n):
        def begin(s, u):
            c_y(s).start()

            @pl.when(zl == line - 1)
            def _():
                c_za(s).start()

            @pl.when(zl == 0)
            def _():
                c_zb(s).start()

        def pair_sum(s, u):
            c_y(s).wait()
            add_in(s, R_OWN, yR)

            @pl.when(zl == line - 1)
            def _():
                c_ya(s).start()

            @pl.when(zl == 0)
            def _():
                c_yb(s).start()

        def line_zb(s, u):
            c_zb(s).wait_recv()
            add_in(s, R_ZB, zZB)

            @pl.when(has_up)
            def _():
                c_zb(s).start()

            @pl.when(zl == line - 1)
            def _():
                c_ex(s, R_ZB).start()

        def line_za(s, u):
            c_za(s).wait_recv()
            add_in(s, R_ZA, zZA)

            @pl.when(has_dn)
            def _():
                c_za(s).start()

            @pl.when(zl == 0)
            def _():
                c_ex(s, R_ZA).start()

        def pair_za(s, u):
            c_ex(s, R_ZA).wait()
            add_in(s, R_ZA, yZ)
            b_za(s).start()

        def pair_zb(s, u):
            c_ex(s, R_ZB).wait()
            add_in(s, R_ZB, yZ)
            b_zb(s).start()

        def line_yb(s, u):
            c_yb(s).wait_recv()
            add_in(s, R_YB, zYB)

            @pl.when(has_up)
            def _():
                c_yb(s).start()

            @pl.when(zl == line - 1)
            def _():
                b_yb(s).start()

        def line_ya(s, u):
            c_ya(s).wait_recv()
            add_in(s, R_YA, zYA)

            @pl.when(has_dn)
            def _():
                c_ya(s).start()

            @pl.when(zl == 0)
            def _():
                b_ya(s).start()

        def back_a(s, u):
            c_za(s).wait_send()
            c_ya(s).wait_send()
            b_za(s).wait_recv()
            b_ya(s).wait_recv()
            part[at(s, R_ZA), :] = zZA[s[1]]
            part[at(s, R_YA), :] = zYA[s[1]]

            @pl.when(has_up)
            def _():
                b_za(s).start()
                b_ya(s).start()

        def back_b(s, u):
            c_zb(s).wait_send()
            c_yb(s).wait_send()
            b_zb(s).wait_recv()
            b_yb(s).wait_recv()
            part[at(s, R_ZB), :] = zZB[s[1]]
            part[at(s, R_YB), :] = zYB[s[1]]

            @pl.when(has_dn)
            def _():
                b_zb(s).start()
                b_yb(s).start()

        def back_pair(s, u):
            b_y(s).start()

        def finish(s, u):
            b_y(s).wait_recv()
            out_copy(s, u).start()

        def drain(s, u):
            out_copy(s, u).wait()
            b_y(s).wait_send()

            @pl.when(has_up)
            def _():
                for item in (b_ya, b_za):
                    item(s).wait_send()

            @pl.when(has_dn)
            def _():
                for item in (b_yb, b_zb):
                    item(s).wait_send()

        on(n, None, begin)
        on(n - line, zl == 0, pair_za)
        on(n - zl, has_dn, line_zb)
        on(n - (line - 1 - zl), has_up, line_za)
        on(n - 1, None, pair_sum)
        on(n - line, zl == line - 1, pair_zb)
        on(n - 1 - zl, has_dn, line_yb)
        on(n - line + zl, has_up, line_ya)
        on(n - line - zl, has_dn, back_a)
        on(n - line - (line - 1 - zl), has_up, back_b)
        on(n - 2 * line + 1, None, back_pair)
        on(n - 2 * line, None, finish)
        on(n - 2 * line - 1, None, drain)

    shared = lax.broadcasted_iota(jnp.int32, (8, width), 0) < 6

    def s_copy(i, src, dst, dev):
        return rcopy(src, dst, sm_s.at[i], sm_r.at[i], dev)

    def small_step(n):
        core = s_copy(0, small, smr.at[0], core_dev)
        across = s_copy(1, small, smr.at[1], x_dev)
        pair = s_copy(2, small, smr.at[2], y_dev)
        down = s_copy(3, small, smr.at[3], dn_dev)
        back = s_copy(4, small, smr.at[4], up_dev)

        def when(m, cond, fn):
            ok = n == small_at + m
            if cond is not None:
                ok = ok & cond
            pl.when(ok)(fn)

        def s0():
            core.start()

        def s1():
            core.wait()
            small[...] = small[...] + jnp.where(shared, smr[0], 0.0)
            across.start()

        def s2():
            across.wait()
            small[...] = small[...] + jnp.where(shared, smr[1], 0.0)
            pair.start()

        def s3():
            pair.wait()
            small[...] = small[...] + smr[2]

            @pl.when(zl == line - 1)
            def _():
                down.start()

        def s4():
            down.wait_recv()
            small[...] = small[...] + smr[3]

            @pl.when(has_dn)
            def _():
                down.start()

            @pl.when(zl == 0)
            def _():
                back.start()

        def s5():
            back.wait_recv()

            @pl.when(has_dn & (zl > 0))
            def _():
                down.wait_send()

            small[...] = smr[4]

            @pl.when(has_up)
            def _():
                back.start()

        when(0, None, s0)
        when(1, None, s1)
        when(2, None, s2)
        when(3, None, s3)
        when(3 + line - 1 - zl, has_up, s4)
        when(3 + line - 1 + zl, has_dn, s5)

    def steps(lo_n, hi_n):
        def body(n, _):
            step(n)
            small_step(n)
            return 0

        lax.fori_loop(lo_n, hi_n, body, 0)

    keys = lax.broadcasted_iota(jnp.int32, (LEN, 128), 0)
    bias[...] = jnp.where(keys < len_ref[0], 0.0, -1e30)
    gain_one, shift_one = gain_1[...].reshape(1, width), shift_1[...].reshape(1, width)
    gain_two, shift_two = gain_2[...].reshape(1, width), shift_2[...].reshape(1, width)
    bias_out, bias_down = b_out[...].reshape(1, width), b_down[...].reshape(1, width)
    CH = 32

    def norm_one(i, _):
        r = pl.ds(pl.multiple_of(i * CH, CH), CH)
        n, _s = norm_parts(tok[r, :].astype(F32))
        first[pl.ds(pl.multiple_of(t * rows + i * CH, CH), CH), :] = (n * gain_one + shift_one).astype(BF)
        return 0

    gather_first = Gather(first, 0)
    lax.fori_loop(0, hrows // CH, norm_one, 0)
    pl.semaphore_wait(barrier, 3 + has_up.astype(jnp.int32) + has_dn.astype(jnp.int32))
    gather_first.x[0].start()
    lax.fori_loop(hrows // CH, rows // CH, norm_one, 0)
    gather_first.x[1].start()
    gather_first.c.start()
    own_cot = pltpu.make_async_copy(cot, cotg.at[blk(t), :], wsem.at[4])
    own_cot.start()
    loads[0].wait()

    cols_qkv = 3 * heads * HD

    def project(b):
        f = first[blk(b), :]
        for base in range(0, cols_qkv, 384):
            w = min(384, cols_qkv - base)
            mixed = dot(f, win[base : base + w, :], 1, 1)
            for i in range(base // HD, (base + w) // HD):
                which, h = i // heads, i % heads
                piece = mixed[:, i * HD - base : (i + 1) * HD - base]
                if which != 1:
                    row = which // 2
                    piece = piece + b_in[row : row + 1, h * HD : (h + 1) * HD]
                piece = piece.astype(BF)
                qkv[i, blk(b), :] = piece
                if which == 1:
                    kt[h, :, blk(b)] = piece.T
                if which == 2:
                    vt[h, :, blk(b)] = piece.T

    project(t)
    gather_first.near()
    project(cp)
    gather_first.far()
    own_cot.wait()
    gather_cot = Gather(cotg, 1)
    gather_cot.start()
    project(xp)
    gather_first.diag()
    project(dg)
    keep_first = pltpu.make_async_copy(first, first_h, wsem.at[5])
    keep_first.start()

    HALF = 2 * rows
    SCALE = HD**-0.5

    def half(i):
        return pl.ds(pl.multiple_of(i * HALF, HALF), HALF)

    def attend(i):
        def head(h, _):
            q = qkv[h, half(i), :]
            k = qkv[heads + h]
            s = dot(k, q, 1, 1) * (SCALE * LOG2E) + bias[:, 0:1]
            top = jnp.max(s, axis=0, keepdims=True)
            p = jnp.exp2(s - top)
            total = jnp.sum(p, axis=0, keepdims=True)
            o = dot(vt[h], p.astype(BF), 1, 0) / total
            ctxT[pl.ds(pl.multiple_of(h * HD, HD), HD), half(i)] = o.astype(BF)
            lse[h, i] = top + jnp.log2(total)
            return 0

        lax.fori_loop(0, heads, head, 0)

    def tiles(n_cols, fn):
        for c0 in range(0, n_cols, 256):
            fn(slice(c0, c0 + 256))

    def project_out(b, put):
        left = ctxT[:, blk(b)]
        tiles(width, lambda c: put(c, dot(left, wout[:, c], 0, 0)))

    loads[1].wait()
    attend(1 - chip)
    sum_out = Scatter(0, 0)
    sum_out.far(project_out)
    attend(chip)
    gather_cot.near()
    gather_cot.far()
    sum_out.close(project_out, mid)
    sum_out.c.wait_recv()
    sum_out.x[0].wait_recv()

    def norm_two(i, _):
        r = pl.ds(pl.multiple_of(i * CH, CH), CH)
        v = tok[r, :].astype(F32) + (mid[r, :] + sum_out.extra(r) + bias_out)
        mid[r, :] = v
        n, _s = norm_parts(v)
        sec[pl.ds(pl.multiple_of(t * rows + i * CH, CH), CH), :] = (n * gain_two + shift_two).astype(BF)
        return 0

    keep_first.wait()
    gather_first.drain()
    gather_sec = Gather(sec, 2)
    lax.fori_loop(0, hrows // CH, norm_two, 0)
    gather_sec.x[0].start()
    sum_out.x[1].wait_recv()
    lax.fori_loop(hrows // CH, rows // CH, norm_two, 0)
    gather_sec.x[1].start()
    gather_sec.c.start()
    sum_out.drain()
    gather_cot.diag()
    loads[2].wait()
    loads[3].wait()

    small[...] = jnp.zeros((8, width), F32)
    f_cols = wup.shape[1]

    def feed_cols(b, c):
        hid = dot(sec[blk(b), :], wup[:, c], 1, 0) + b_up[c].reshape(1, 256)
        phi = 0.5 * (1.0 + lax.erf(hid * 0.7071067811865476))
        act[blk(b), c] = (hid * phi).astype(BF)
        slope = phi + hid * (0.3989422804014327 * jnp.exp(hid * hid * -0.5))
        grad = (dot(cotg[blk(b), :], wdown[c, :], 1, 1) * slope).astype(BF)
        gh[blk(b), c] = grad
        small[6:7, c] = small[6:7, c] + jnp.sum(grad.astype(F32), axis=0, keepdims=True)

    def chunk(i):
        return pl.ds(pl.multiple_of(i * 256, 256), 256)

    def feed(b):
        def cols(i, _):
            feed_cols(b, chunk(i))
            return 0

        lax.fori_loop(0, f_cols // 256, cols, 0)

    def weight_rows(base, left, c, right):
        lhs = left[:, c]
        r = pl.ds(pl.multiple_of(base, 64), lhs.shape[1])
        tiles(width, lambda cc: part.__setitem__((r, cc), dot(lhs, right[:, cc], 0, 0).astype(BF)))

    feed(t)
    gather_sec.near()
    feed(cp)
    gather_sec.far()
    gather_sec.diag()

    n_feed = f_cols // 256
    n_up = width // 256

    def feed_far(i, _):
        feed_cols(xp, chunk(i))
        feed_cols(dg, chunk(i))
        weight_rows(i * 256, act, chunk(i), cotg)
        step(i)
        return 0

    lax.fori_loop(0, n_feed, feed_far, 0)

    def back_up(b, put):
        left = gh[blk(b), :]
        tiles(width, lambda c: put(c, dot(left, wup[c, :], 1, 1)))

    sum_sec = Scatter(1, 1)
    sum_sec.far(back_up)
    step(n_feed)
    sum_sec.close(back_up, gmid)
    step(n_feed + 1)
    now = n_feed + 2

    def up_rows(i, _):
        weight_rows(f_cols + i * 256, sec, chunk(i), gh)

        @pl.when(i >= n_up - 2)
        def _():
            step(now + i - (n_up - 2))

        return 0

    lax.fori_loop(0, n_up, up_rows, 0)
    sum_sec.wait()
    now = now + 2

    zero_rows = jnp.zeros((1, width), F32)

    def total(v):
        return jnp.sum(v, axis=0, keepdims=True)

    def middle_back(i, carry):
        d_gain, d_shift, d_out, d_down = carry
        r = pl.ds(pl.multiple_of(i * CH, CH), CH)
        e = gmid[r, :] + sum_sec.extra(r)
        n, scale = norm_parts(mid[r, :])
        tt = e * gain_two
        inner = (tt - jnp.mean(tt, -1, keepdims=True) - n * jnp.mean(tt * n, -1, keepdims=True)) * scale
        c_rows = cot[r, :].astype(F32)
        gm = c_rows + inner
        gmid[r, :] = gm
        low = gm.astype(BF)
        branch[pl.ds(pl.multiple_of(t * rows + i * CH, CH), CH), :] = low
        return (
            d_gain + total(e * n), d_shift + total(e), d_out + total(low.astype(F32)), d_down + total(c_rows)
        )

    d_gain, d_shift, d_out, d_down = lax.fori_loop(0, rows // CH, middle_back, (zero_rows,) * 4)
    small[3:4, :] = d_gain
    small[4:5, :] = d_shift
    small[2:3, :] = d_out
    small[5:6, :] = d_down
    gather_branch = Gather(branch, 3)
    gather_branch.start()
    sum_sec.drain()
    step(now)

    def down(b, put):
        left = act[blk(b), :]
        tiles(width, lambda c: put(c, dot(left, wdown[:, c], 1, 0)))

    sum_down = Scatter(2, 0)
    sum_down.far(down, send=False)
    step(now + 1)
    sum_down.close(down, lo)
    load_first = pltpu.make_async_copy(first_h, first2, wsem.at[6])
    load_first.start()
    step(now + 2)
    now = now + 3

    def back_out(b):
        grad = dot(branch[blk(b), :], wout[...], 1, 1).astype(BF)
        for h in range(heads):
            dO[h, blk(b), :] = grad[:, h * HD : (h + 1) * HD]

    back_out(t)
    gather_branch.near()
    back_out(cp)
    gather_branch.far()
    sum_down.send()
    back_out(xp)
    gather_branch.diag()
    back_out(dg)
    step(now)
    now = now + 1

    def attend_back(h, _):
        k = qkv[heads + h]
        v = qkv[2 * heads + h]
        for i in range(LEN // HALF):
            r = slice(i * HALF, (i + 1) * HALF)
            q = qkv[h, r, :]
            o_grad = dO[h, r, :]
            s = dot(k, q, 1, 1) * (SCALE * LOG2E) + bias[:, 0:1]
            p = jnp.exp2(s - lse[h, i])
            dp = dot(v, o_grad, 1, 1)
            delta = jnp.sum(p * dp, axis=0, keepdims=True)
            ds = (p * (dp - delta)).astype(BF)
            d_v = dot(p.astype(BF), o_grad, 1, 0)
            d_k = dot(ds, q, 1, 0)
            if i == 0:
                dv[...] = d_v
                dk[...] = d_k
            else:
                dv[...] = dv[...] + d_v
                dk[...] = dk[...] + d_k
            d_q = dot(kt[h], ds, 1, 0) * SCALE
            qkv[h, r, :] = d_q.T.astype(BF)
        qkv[heads + h] = (dk[...] * SCALE).astype(BF)
        qkv[2 * heads + h] = dv[...].astype(BF)
        step(now + h)
        return 0

    lax.fori_loop(0, heads, attend_back, 0)
    now = now + heads
    assert now <= ring

    def assemble(i, carry):
        r = pl.ds(pl.multiple_of(i * 256, 256), 256)
        for p in range(3 * heads):
            dmx[r, p * HD : (p + 1) * HD] = qkv[p, r, :]
        return carry + total(dmx[r, 0:cols_qkv].astype(F32))

    gather_sec.drain()
    small[7:8, 0:cols_qkv] = lax.fori_loop(0, LEN // 256, assemble, jnp.zeros((1, cols_qkv), F32))

    def back_first(b, put):
        left = dmx[blk(b), 0:cols_qkv]
        tiles(width, lambda c: put(c, dot(left, win[:, c], 1, 0)))

    sum_down.drain()
    sum_first = Scatter(3, 1)
    sum_first.far(back_first)
    step(now)
    sum_first.close(back_first, gtok)
    now = now + 1
    load_first.wait()

    def finish_out(i, _):
        r = pl.ds(pl.multiple_of(i * CH, CH), CH)
        lo[r, :] = mid[r, :] + lo[r, :] + sum_down.extra(r) + bias_down
        return 0

    def tokens_back(i, carry):
        d_gain, d_shift = carry
        r = pl.ds(pl.multiple_of(i * CH, CH), CH)
        e = gtok[r, :] + sum_first.extra(r)
        n, scale = norm_parts(tok[r, :].astype(F32))
        tt = e * gain_one
        inner = (tt - jnp.mean(tt, -1, keepdims=True) - n * jnp.mean(tt * n, -1, keepdims=True)) * scale
        gtok[r, :] = gmid[r, :] + inner
        return (d_gain + total(e * n), d_shift + total(e))

    steps(now, start_of(ring))
    put_lo = pltpu.make_async_copy(lo, lo_h, wsem.at[7])
    put_gtok = pltpu.make_async_copy(gtok, gtok_h, wsem.at[8])
    now = start_of(ring)
    all_rows = cols_qkv + heads * HD
    for base in range(0, all_rows, 256):
        top = min(base + 256, all_rows)
        if base < cols_qkv:
            weight_rows(base, dmx, slice(base, min(top, cols_qkv)), first2)
        if top > cols_qkv:
            o0 = max(base, cols_qkv)
            left = ctxT[o0 - cols_qkv : top - cols_qkv, :]
            tiles(width, lambda c: part.__setitem__((slice(o0, top), c), dot(left, branch[:, c], 1, 0).astype(BF)))
        upto = start_of(ring + top // UNIT - 1) + 1
        steps(now, upto)
        now = upto
        if base == 512:
            sum_first.wait()
            d_gain, d_shift = lax.fori_loop(0, rows // CH, tokens_back, (zero_rows,) * 2)
            small[0:1, :] = d_gain
            small[1:2, :] = d_shift
            put_gtok.start()
        if base == 768:
            sum_down.wait()
            lax.fori_loop(0, rows // CH, finish_out, 0)
            put_lo.start()
    steps(now, last)
    put_lo.wait()
    put_gtok.wait()

    gather_cot.drain()
    gather_branch.drain()
    sum_first.drain()

    @pl.when(has_up)
    def _():
        s_copy(4, small, smr.at[4], up_dev).wait_send()


def widen(counts, gout, lo, gtok, small, *refs):
    outs, (lo_o, gtok_o), vectors, gb_in = refs[:4], refs[4:6], refs[6:13], refs[13]
    held, full, two, sems = refs[14:]
    tile = 128
    copies = []
    at = 0
    for count, out in zip(counts, outs):
        for start in range(0, count, tile):
            r = slice(at + start, at + min(start + tile, count))
            dst = slice(start, min(start + tile, count))
            copies.append((r, out.at[dst, :]))
        at = at + count
    fetch = [pltpu.make_async_copy(src, two.at[i], sems.at[i]) for i, src in enumerate((lo, gtok))]
    moves = [pltpu.make_async_copy(two.at[i], dst, sems.at[i]) for i, dst in enumerate((lo_o, gtok_o))]
    loads = [
        pltpu.make_async_copy(gout.at[r, :], held.at[r, :], sems.at[2 + 2 * i]) for i, (r, _) in enumerate(copies)
    ]
    stores = [pltpu.make_async_copy(full.at[r, :], out, sems.at[3 + 2 * i]) for i, (r, out) in enumerate(copies)]
    for item in fetch + loads:
        item.start()
    for i, out in enumerate(vectors):
        out[...] = small[i, :]
    cols = gb_in.shape[1]
    gb_in[0:1, :] = small[7:8, 0:cols]
    gb_in[1:2, :] = small[7:8, 2 * cols : 3 * cols]
    for item, move in zip(fetch, moves):
        item.wait()
        move.start()
    for (r, _), load, store in zip(copies, loads, stores):
        load.wait()
        full[r, :] = held[r, :].astype(F32)
        store.start()
    for item in stores + moves:
        item.wait()


def solution(mesh):
    n_dp = mesh.shape["dp"]

    def local(tokens, lengths, gain_one, shift_one, weight_in, bias_in, weight_out, bias_out, gain_two, shift_two,
              weight_up, bias_up, weight_down, bias_down, cotangent):
        rows, width = tokens.shape
        cols = weight_in.shape[2]
        heads = cols // HD
        f_cols = weight_up.shape[1]
        w_in = weight_in.transpose(1, 2, 0).reshape(3 * cols, width)
        total = 4 * rows
        g_rows = f_cols + width + 4 * cols
        ring = (f_cols + width) // UNIT
        vm = pl.BlockSpec(memory_space=pltpu.VMEM)
        hb = pl.BlockSpec(memory_space=pl.ANY)
        big = pltpu.VMEM((total, width), BF)
        lo, gtok, small, gout, _first = pl.pallas_call(
            functools.partial(kernel, n_dp),
            out_shape=[
                jax.ShapeDtypeStruct((rows, width), F32),
                jax.ShapeDtypeStruct((rows, width), F32),
                jax.ShapeDtypeStruct((8, width), F32),
                jax.ShapeDtypeStruct((g_rows, width), BF),
                jax.ShapeDtypeStruct((total, width), BF),
            ],
            in_specs=[pl.BlockSpec(memory_space=pltpu.SMEM)] + [vm] * 10 + [hb] * 4,
            out_specs=[hb, hb, vm, hb, hb],
            scratch_shapes=[
                pltpu.VMEM((rows, width), F32),
                pltpu.VMEM((rows, width), F32),
                pltpu.VMEM((3 * cols, width), BF),
                pltpu.VMEM((cols, width), BF),
                pltpu.VMEM((width, f_cols), BF),
                pltpu.VMEM((f_cols, width), BF),
                big, big, big,
                pltpu.VMEM((total, f_cols), BF),
                pltpu.VMEM((total, f_cols), BF),
                pltpu.VMEM((3 * heads, LEN, HD), BF),
                pltpu.VMEM((heads, HD, LEN), BF),
                pltpu.VMEM((heads, HD, LEN), BF),
                pltpu.VMEM((cols, LEN), BF),
                pltpu.VMEM((heads, LEN, HD), BF),
                pltpu.VMEM((LEN, HD), F32),
                pltpu.VMEM((LEN, HD), F32),
                pltpu.VMEM((rows, width), F32),
                pltpu.VMEM((rows, width), F32),
                pltpu.VMEM((LEN, 128), F32),
                pltpu.VMEM((heads, 2, 1, 2 * rows), F32),
                pltpu.VMEM((3, rows, width), BF),
                pltpu.VMEM((2, 3, rows, width), BF),
                pltpu.VMEM((ring * UNIT, width), BF),
                pltpu.VMEM((SLOTS, YH, width), BF),
                pltpu.VMEM((SLOTS, YF, width), BF),
                pltpu.VMEM((SLOTS, YF, width), BF),
                pltpu.VMEM((SLOTS, ZF, width), BF),
                pltpu.VMEM((SLOTS, ZF, width), BF),
                pltpu.VMEM((SLOTS, ZF, width), BF),
                pltpu.VMEM((5, 8, width), F32),
                pltpu.SemaphoreType.DMA((9,)),
                pltpu.SemaphoreType.DMA((4, 5)),
                pltpu.SemaphoreType.DMA((4, 5)),
                pltpu.SemaphoreType.DMA((4, 4)),
                pltpu.SemaphoreType.DMA((4, 4)),
                pltpu.SemaphoreType.DMA((KINDS, SLOTS)),
                pltpu.SemaphoreType.DMA((KINDS, SLOTS)),
                pltpu.SemaphoreType.DMA((SLOTS,)),
                pltpu.SemaphoreType.DMA((5,)),
                pltpu.SemaphoreType.DMA((5,)),
            ],
            compiler_params=pltpu.CompilerParams(
                collective_id=0, has_side_effects=True, vmem_limit_bytes=HIGH
            ),
        )(lengths, tokens, cotangent, gain_one, shift_one, bias_out, gain_two, shift_two, bias_down, bias_up, bias_in,
          w_in, weight_out, weight_up, weight_down)
        flat = jax.ShapeDtypeStruct((width,), F32)
        wide = [f_cols, width, 3 * cols, cols]
        outs = pl.pallas_call(
            functools.partial(widen, wide),
            out_shape=[jax.ShapeDtypeStruct((n, width), F32) for n in wide]
            + [jax.ShapeDtypeStruct((rows, width), F32)] * 2
            + [flat] * 7
            + [jax.ShapeDtypeStruct((2, cols), F32)],
            in_specs=[hb, hb, hb, vm],
            out_specs=[hb] * 6 + [vm] * 8,
            scratch_shapes=[
                pltpu.VMEM((g_rows, width), BF),
                pltpu.VMEM((g_rows, width), F32),
                pltpu.VMEM((2, rows, width), F32),
                pltpu.SemaphoreType.DMA((2 * (g_rows // 128 + 4) + 2,)),
            ],
            compiler_params=pltpu.CompilerParams(vmem_limit_bytes=HIGH),
        )(gout, lo, gtok, small)
        g_down, g_up, g_in, g_out, lo, gtok, gg1, gs1, gb_out, gg2, gs2, gb_down, gb_up, gb_in = outs
        g_in = g_in.reshape(3, cols, width).transpose(2, 0, 1)
        return (lo, gtok, gg1, gs1, g_in, gb_in, g_out, gb_out, gg2, gs2, g_up, gb_up, g_down, gb_down)

    rows2 = P(("dp", "tensor"), None)
    every = P()
    return jax.shard_map(
        local,
        mesh=mesh,
        in_specs=(rows2, P("dp"), every, every, P(None, None, "tensor"), P(None, "tensor"), P("tensor", None), every,
                  every, every, P(None, "tensor"), P("tensor"), P("tensor", None), every, rows2),
        out_specs=(rows2, rows2, every, every, P(None, None, "tensor"), P(None, "tensor"), P("tensor", None), every,
                   every, every, P(None, "tensor"), P("tensor"), P("tensor", None), every),
        check_vma=False,
    )
```

```python
import functools

import jax
import jax.numpy as jnp
from jax import lax
from jax.experimental import pallas as pl
from jax.experimental.pallas import tpu as pltpu
from jax.sharding import PartitionSpec as P

HD = 64
LEN = 1024
BF = jnp.bfloat16
F32 = jnp.float32
MESH = pl.DeviceIdType.MESH
LOG2E = 1.4426950408889634
LN2 = 0.6931471805599453
UNIT = 128
YH = UNIT // 4
YF = UNIT // 8
ZF = UNIT // 4
ZA0 = UNIT // 2
ZB0 = ZA0 + ZF
KINDS = 7
SLOTS = 10
HIGH = 62 * 2**20


def dot(left, right, left_dim, right_dim):
    return lax.dot_general(
        left, right, (((left_dim,), (right_dim,)), ((), ())), preferred_element_type=F32
    )


def norm_parts(rows):
    centre = rows - jnp.mean(rows, axis=-1, keepdims=True)
    scale = lax.rsqrt(jnp.mean(centre * centre, axis=-1, keepdims=True) + 1e-05)
    return centre * scale, scale


def kernel(n_dp, len_ref, tok, cot, gain_1, shift_1, b_out, gain_2, shift_2, b_down, b_up, b_in, win_h, wout_h, wup_h, wdown_h,
           lo_h, gtok_h, small, gout, first_h,
           lo, gtok, win, wout, wup, wdown, first, cotg, sec, act, gh,
           qkv, vt, kt, ctxT, dO, dk, dv, mid, gmid, bias, lse,
           ps, rcv, part, yR, zYA, zYB, zZA, zZB, yZ, smr,
           wsem, ag_s, ag_r, rs_s, rs_r, dp_s, dp_r, out_s, sm_s, sm_r):
    line = n_dp // 2
    width = tok.shape[1]
    rows = tok.shape[0]
    heads = dO.shape[0]
    units = gout.shape[0] // UNIT
    ring = part.shape[0] // UNIT
    gap = max(0, 2 * line + 2 - SLOTS)

    def start_of(u):
        return u + gap * (u // SLOTS)

    small_at = start_of(units - 3)
    last = start_of(units - 1) + 2 * line + 2
    branch = first
    first2 = act
    dmx = sec

    g = lax.axis_index("dp")
    t = lax.axis_index("tensor")
    cp = t + 1 - 2 * lax.rem(t, 2)
    xp = lax.rem(t + 2, 4)
    dg = lax.rem(cp + 2, 4)
    y = lax.rem(g, 2)
    zl = lax.div(g, 2)
    chip = lax.div(t, 2)
    core_dev = (g, cp)
    x_dev = (g, xp)
    y_dev = (g + 1 - 2 * y, t)
    up_dev = (g + 2, t)
    dn_dev = (g - 2, t)
    has_up = zl < line - 1
    has_dn = zl > 0

    def blk(b):
        return pl.ds(pl.multiple_of(b * rows, rows), rows)

    def rcopy(src, dst, s_sem, r_sem, dev):
        return pltpu.make_async_remote_copy(
            src_ref=src, dst_ref=dst, send_sem=s_sem, recv_sem=r_sem, device_id=dev, device_id_type=MESH
        )

    loads = [
        pltpu.make_async_copy(win_h, win, wsem.at[0]),
        pltpu.make_async_copy(wout_h, wout, wsem.at[1]),
        pltpu.make_async_copy(wup_h, wup, wsem.at[2]),
        pltpu.make_async_copy(wdown_h, wdown, wsem.at[3]),
    ]
    own_cot = pltpu.make_async_copy(cot, cotg.at[pl.ds(pl.multiple_of(t * rows, rows), rows), :], wsem.at[4])
    loads[0].start()
    own_cot.start()
    for item in loads[1:]:
        item.start()

    barrier = pltpu.get_barrier_semaphore()
    for dev in (core_dev, x_dev, y_dev):
        pl.semaphore_signal(barrier, inc=1, device_id=dev, device_id_type=MESH)

    @pl.when(has_up)
    def _():
        pl.semaphore_signal(barrier, inc=1, device_id=up_dev, device_id_type=MESH)

    @pl.when(has_dn)
    def _():
        pl.semaphore_signal(barrier, inc=1, device_id=dn_dev, device_id_type=MESH)

    hrows = rows // 2

    def piece_rows(b, i):
        return pl.ds(pl.multiple_of(b * rows + i * hrows, hrows), hrows)

    class Gather:
        def __init__(self, buf, at):
            own = buf.at[blk(t), :]
            self.c = rcopy(own, own, ag_s.at[at, 4], ag_r.at[at, 4], core_dev)
            self.x, self.f = [], []
            for i in range(2):
                mine, theirs = buf.at[piece_rows(t, i), :], buf.at[piece_rows(xp, i), :]
                self.x.append(rcopy(mine, mine, ag_s.at[at, i], ag_r.at[at, i], x_dev))
                self.f.append(rcopy(theirs, theirs, ag_s.at[at, 2 + i], ag_r.at[at, 2 + i], core_dev))

        def start(self):
            self.x[0].start()
            self.x[1].start()
            self.c.start()

        def drain(self):
            for item in self.x + [self.c] + self.f:
                item.wait_send()

        def near(self):
            self.c.wait_recv()

        def far(self):
            for i in range(2):
                self.x[i].wait_recv()
                self.f[i].start()

        def diag(self):
            self.f[0].wait_recv()
            self.f[1].wait_recv()

    class Scatter:
        def __init__(self, at, slot):
            self.own_in, self.x_relay, self.x_in = (rcv.at[slot, i] for i in range(3))
            self.d = rcopy(ps.at[0], rcv.at[slot, 1], rs_s.at[at, 0], rs_r.at[at, 0], core_dev)
            self.x = []
            for i in range(2):
                r = pl.ds(i * hrows, hrows)
                self.x.append(
                    rcopy(ps.at[1, r, :], rcv.at[slot, 2, r, :], rs_s.at[at, 2 + i], rs_r.at[at, 2 + i], x_dev)
                )
            self.c = rcopy(ps.at[2], rcv.at[slot, 0], rs_s.at[at, 1], rs_r.at[at, 1], core_dev)

        def far(self, fn, send=True):
            fn(dg, functools.partial(self.put, 0))
            self.d.start()
            fn(xp, functools.partial(self.put, 1))
            self.d.wait_recv()

            def add(i, _):
                r = pl.ds(pl.multiple_of(i * 64, 64), 64)
                ps[1, r, :] = (ps[1, r, :].astype(F32) + self.x_relay[r, :].astype(F32)).astype(BF)
                return 0

            lax.fori_loop(0, rows // 64, add, 0)
            if send:
                self.send()

        def send(self):
            self.x[0].start()
            self.x[1].start()

        @staticmethod
        def put(slot, cols, value):
            ps[slot, :, cols] = value.astype(BF)

        def close(self, fn, total):
            fn(cp, functools.partial(self.put, 2))
            self.c.start()

            def keep(cols, value):
                total[:, cols] = value

            fn(t, keep)

        def wait(self):
            self.c.wait_recv()
            self.x[0].wait_recv()
            self.x[1].wait_recv()

        def extra(self, r):
            return self.own_in[r, :].astype(F32) + self.x_in[r, :].astype(F32)

        def drain(self):
            for item in [self.d, self.c] + self.x:
                item.wait_send()

    def unit_of(m):
        if gap == 0:
            return (m >= 0) & (m < units), m
        r = lax.rem(m, SLOTS + gap)
        u = lax.div(m, SLOTS + gap) * SLOTS + r
        return (m >= 0) & (r < SLOTS) & (u < units), u

    R_OWN, R_OTHER = (y * YH, YH), ((1 - y) * YH, YH)
    R_YA, R_YB = (y * YH, YF), (y * YH + YF, YF)
    R_ZA, R_ZB = (ZA0, ZF), (ZB0, ZF)

    def at(s, where):
        start, count = where
        return pl.ds(pl.multiple_of(s[0] * UNIT + start, count), count)

    def dcopy(kind, s, src_rows, dst, dev):
        return rcopy(part.at[at(s, src_rows), :], dst, dp_s.at[kind, s[1]], dp_r.at[kind, s[1]], dev)

    def c_y(s):
        return dcopy(0, s, R_OTHER, yR.at[s[1]], y_dev)

    def c_ya(s):
        return dcopy(1, s, R_YA, zYA.at[s[1]], dn_dev)

    def c_yb(s):
        return dcopy(2, s, R_YB, zYB.at[s[1]], up_dev)

    def c_za(s):
        return dcopy(3, s, R_ZA, zZA.at[s[1]], dn_dev)

    def c_zb(s):
        return dcopy(4, s, R_ZB, zZB.at[s[1]], up_dev)

    def c_ex(s, which):
        return dcopy(5, s, which, yZ.at[s[1]], y_dev)

    def b_ya(s):
        return dcopy(1, s, R_YA, zYA.at[s[1]], up_dev)

    def b_yb(s):
        return dcopy(2, s, R_YB, zYB.at[s[1]], dn_dev)

    def b_y(s):
        return dcopy(6, s, R_OWN, part.at[at(s, R_OWN), :], y_dev)

    def b_za(s):
        return dcopy(3, s, R_ZA, zZA.at[s[1]], up_dev)

    def b_zb(s):
        return dcopy(4, s, R_ZB, zZB.at[s[1]], dn_dev)

    def add_in(s, where, got):
        r = at(s, where)
        part[r, :] = (part[r, :].astype(F32) + got[s[1]].astype(F32)).astype(BF)

    def out_copy(s, u):
        return pltpu.make_async_copy(
            part.at[at(s, (0, UNIT)), :], gout.at[pl.ds(pl.multiple_of(u * UNIT, UNIT), UNIT), :], out_s.at[s[1]]
        )

    def on(m, cond, fn):
        ok, u = unit_of(m)
        if cond is not None:
            ok = ok & cond

        @pl.when(ok)
        def _():
            fn((lax.rem(u, ring), lax.rem(u, SLOTS)), u)

    def step(n):
        def begin(s, u):
            c_y(s).start()

            @pl.when(zl == line - 1)
            def _():
                c_za(s).start()

            @pl.when(zl == 0)
            def _():
                c_zb(s).start()

        def pair_sum(s, u):
            c_y(s).wait()
            add_in(s, R_OWN, yR)

            @pl.when(zl == line - 1)
            def _():
                c_ya(s).start()

            @pl.when(zl == 0)
            def _():
                c_yb(s).start()

        def line_zb(s, u):
            c_zb(s).wait_recv()
            add_in(s, R_ZB, zZB)

            @pl.when(has_up)
            def _():
                c_zb(s).start()

            @pl.when(zl == line - 1)
            def _():
                c_ex(s, R_ZB).start()

        def line_za(s, u):
            c_za(s).wait_recv()
            add_in(s, R_ZA, zZA)

            @pl.when(has_dn)
            def _():
                c_za(s).start()

            @pl.when(zl == 0)
            def _():
                c_ex(s, R_ZA).start()

        def pair_za(s, u):
            c_ex(s, R_ZA).wait()
            add_in(s, R_ZA, yZ)
            b_za(s).start()

        def pair_zb(s, u):
            c_ex(s, R_ZB).wait()
            add_in(s, R_ZB, yZ)
            b_zb(s).start()

        def line_yb(s, u):
            c_yb(s).wait_recv()
            add_in(s, R_YB, zYB)

            @pl.when(has_up)
            def _():
                c_yb(s).start()

            @pl.when(zl == line - 1)
            def _():
                b_yb(s).start()

        def line_ya(s, u):
            c_ya(s).wait_recv()
            add_in(s, R_YA, zYA)

            @pl.when(has_dn)
            def _():
                c_ya(s).start()

            @pl.when(zl == 0)
            def _():
                b_ya(s).start()

        def back_a(s, u):
            c_za(s).wait_send()
            c_ya(s).wait_send()
            b_za(s).wait_recv()
            b_ya(s).wait_recv()
            part[at(s, R_ZA), :] = zZA[s[1]]
            part[at(s, R_YA), :] = zYA[s[1]]

            @pl.when(has_up)
            def _():
                b_za(s).start()
                b_ya(s).start()

        def back_b(s, u):
            c_zb(s).wait_send()
            c_yb(s).wait_send()
            b_zb(s).wait_recv()
            b_yb(s).wait_recv()
            part[at(s, R_ZB), :] = zZB[s[1]]
            part[at(s, R_YB), :] = zYB[s[1]]

            @pl.when(has_dn)
            def _():
                b_zb(s).start()
                b_yb(s).start()

        def back_pair(s, u):
            b_y(s).start()

        def finish(s, u):
            b_y(s).wait_recv()
            out_copy(s, u).start()

        def drain(s, u):
            out_copy(s, u).wait()
            b_y(s).wait_send()

            @pl.when(has_up)
            def _():
                for item in (b_ya, b_za):
                    item(s).wait_send()

            @pl.when(has_dn)
            def _():
                for item in (b_yb, b_zb):
                    item(s).wait_send()

        on(n, None, begin)
        on(n - line, zl == 0, pair_za)
        on(n - zl, has_dn, line_zb)
        on(n - (line - 1 - zl), has_up, line_za)
        on(n - 1, None, pair_sum)
        on(n - line, zl == line - 1, pair_zb)
        on(n - 1 - zl, has_dn, line_yb)
        on(n - line + zl, has_up, line_ya)
        on(n - line - zl, has_dn, back_a)
        on(n - line - (line - 1 - zl), has_up, back_b)
        on(n - 2 * line + 1, None, back_pair)
        on(n - 2 * line, None, finish)
        on(n - 2 * line - 1, None, drain)

    shared = lax.broadcasted_iota(jnp.int32, (8, width), 0) < 6

    def s_copy(i, src, dst, dev):
        return rcopy(src, dst, sm_s.at[i], sm_r.at[i], dev)

    def small_step(n):
        core = s_copy(0, small, smr.at[0], core_dev)
        across = s_copy(1, small, smr.at[1], x_dev)
        pair = s_copy(2, small, smr.at[2], y_dev)
        down = s_copy(3, small, smr.at[3], dn_dev)
        back = s_copy(4, small, smr.at[4], up_dev)

        def when(m, cond, fn):
            ok = n == small_at + m
            if cond is not None:
                ok = ok & cond
            pl.when(ok)(fn)

        def s0():
            core.start()

        def s1():
            core.wait()
            small[...] = small[...] + jnp.where(shared, smr[0], 0.0)
            across.start()

        def s2():
            across.wait()
            small[...] = small[...] + jnp.where(shared, smr[1], 0.0)
            pair.start()

        def s3():
            pair.wait()
            small[...] = small[...] + smr[2]

            @pl.when(zl == line - 1)
            def _():
                down.start()

        def s4():
            down.wait_recv()
            small[...] = small[...] + smr[3]

            @pl.when(has_dn)
            def _():
                down.start()

            @pl.when(zl == 0)
            def _():
                back.start()

        def s5():
            back.wait_recv()

            @pl.when(has_dn & (zl > 0))
            def _():
                down.wait_send()

            small[...] = smr[4]

            @pl.when(has_up)
            def _():
                back.start()

        when(0, None, s0)
        when(1, None, s1)
        when(2, None, s2)
        when(3, None, s3)
        when(3 + line - 1 - zl, has_up, s4)
        when(3 + line - 1 + zl, has_dn, s5)

    def steps(lo_n, hi_n):
        def body(n, _):
            step(n)
            small_step(n)
            return 0

        lax.fori_loop(lo_n, hi_n, body, 0)

    keys = lax.broadcasted_iota(jnp.int32, (LEN, 128), 0)
    bias[...] = jnp.where(keys < len_ref[0], 0.0, -1e30)
    gain_one, shift_one = gain_1[...].reshape(1, width), shift_1[...].reshape(1, width)
    gain_two, shift_two = gain_2[...].reshape(1, width), shift_2[...].reshape(1, width)
    bias_out, bias_down = b_out[...].reshape(1, width), b_down[...].reshape(1, width)
    CH = 32

    def norm_one(i, _):
        r = pl.ds(pl.multiple_of(i * CH, CH), CH)
        n, _s = norm_parts(tok[r, :].astype(F32))
        first[pl.ds(pl.multiple_of(t * rows + i * CH, CH), CH), :] = (n * gain_one + shift_one).astype(BF)
        return 0

    gather_first = Gather(first, 0)
    lax.fori_loop(0, hrows // CH, norm_one, 0)
    pl.semaphore_wait(barrier, 3 + has_up.astype(jnp.int32) + has_dn.astype(jnp.int32))
    gather_first.x[0].start()
    lax.fori_loop(hrows // CH, rows // CH, norm_one, 0)
    gather_first.x[1].start()
    gather_first.c.start()
    own_cot.wait()
    gather_cot = Gather(cotg, 1)
    gather_cot.start()
    loads[0].wait()

    cols_qkv = 3 * heads * HD

    def project(b):
        f = first[blk(b), :]
        for base in range(0, cols_qkv, 384):
            w = min(384, cols_qkv - base)
            mixed = dot(f, win[base : base + w, :], 1, 1)
            for i in range(base // HD, (base + w) // HD):
                which, h = i // heads, i % heads
                piece = mixed[:, i * HD - base : (i + 1) * HD - base]
                if which != 1:
                    row = which // 2
                    piece = piece + b_in[row : row + 1, h * HD : (h + 1) * HD]
                piece = piece.astype(BF)
                qkv[i, blk(b), :] = piece
                if which == 1:
                    kt[h, :, blk(b)] = piece.T
                if which == 2:
                    vt[h, :, blk(b)] = piece.T

    project(t)
    gather_first.near()
    project(cp)
    gather_first.far()
    project(xp)
    gather_first.diag()
    project(dg)
    keep_first = pltpu.make_async_copy(first, first_h, wsem.at[5])
    keep_first.start()

    HALF = 2 * rows
    SCALE = HD**-0.5

    def half(i):
        return pl.ds(pl.multiple_of(i * HALF, HALF), HALF)

    def attend(i):
        def head(h, _):
            q = qkv[h, half(i), :]
            k = qkv[heads + h]
            s = dot(k, q, 1, 1) * (SCALE * LOG2E) + bias[:, 0:1]
            top = jnp.max(s, axis=0, keepdims=True)
            p = jnp.exp2(s - top)
            total = jnp.sum(p, axis=0, keepdims=True)
            o = dot(vt[h], p.astype(BF), 1, 0) / total
            ctxT[pl.ds(pl.multiple_of(h * HD, HD), HD), half(i)] = o.astype(BF)
            lse[h, i] = top + jnp.log2(total)
            return 0

        lax.fori_loop(0, heads, head, 0)

    def tiles(n_cols, fn):
        for c0 in range(0, n_cols, 256):
            fn(slice(c0, c0 + 256))

    def project_out(b, put):
        left = ctxT[:, blk(b)]
        tiles(width, lambda c: put(c, dot(left, wout[:, c], 0, 0)))

    loads[1].wait()
    attend(1 - chip)
    sum_out = Scatter(0, 0)
    sum_out.far(project_out)
    attend(chip)
    gather_cot.near()
    gather_cot.far()
    sum_out.close(project_out, mid)
    sum_out.c.wait_recv()
    sum_out.x[0].wait_recv()

    def norm_two(i, _):
        r = pl.ds(pl.multiple_of(i * CH, CH), CH)
        v = tok[r, :].astype(F32) + (mid[r, :] + sum_out.extra(r) + bias_out)
        mid[r, :] = v
        n, _s = norm_parts(v)
        sec[pl.ds(pl.multiple_of(t * rows + i * CH, CH), CH), :] = (n * gain_two + shift_two).astype(BF)
        return 0

    keep_first.wait()
    gather_first.drain()
    gather_sec = Gather(sec, 0)
    lax.fori_loop(0, hrows // CH, norm_two, 0)
    gather_sec.x[0].start()
    sum_out.x[1].wait_recv()
    lax.fori_loop(hrows // CH, rows // CH, norm_two, 0)
    gather_sec.x[1].start()
    gather_sec.c.start()
    sum_out.drain()
    gather_cot.diag()
    loads[2].wait()
    loads[3].wait()

    small[...] = jnp.zeros((8, width), F32)
    f_cols = wup.shape[1]

    def activate(b, c):
        hid = dot(sec[blk(b), :], wup[:, c], 1, 0) + b_up[c].reshape(1, 256)
        phi = 0.5 * (1.0 + lax.erf(hid * 0.7071067811865476))
        act[blk(b), c] = (hid * phi).astype(BF)
        return phi + hid * (0.3989422804014327 * jnp.exp(hid * hid * -0.5))

    def hidden_back(b, c, slope):
        grad = (dot(cotg[blk(b), :], wdown[c, :], 1, 1) * slope).astype(BF)
        gh[blk(b), c] = grad
        small[6:7, c] = small[6:7, c] + jnp.sum(grad.astype(F32), axis=0, keepdims=True)

    def chunk(i):
        return pl.ds(pl.multiple_of(i * 256, 256), 256)

    def feed(b):
        def cols(i, _):
            hidden_back(b, chunk(i), activate(b, chunk(i)))
            return 0

        lax.fori_loop(0, f_cols // 256, cols, 0)

    def weight_rows(base, left, c, right):
        lhs = left[:, c]
        r = pl.ds(pl.multiple_of(base, 64), lhs.shape[1])
        tiles(width, lambda cc: part.__setitem__((r, cc), dot(lhs, right[:, cc], 0, 0).astype(BF)))

    feed(t)
    gather_sec.near()
    feed(cp)
    gather_sec.far()
    gather_sec.diag()

    n_feed = f_cols // 256
    n_up = width // 256

    def feed_far(i, _):
        c = chunk(i)
        slope_x, slope_d = activate(xp, c), activate(dg, c)
        weight_rows(i * 256, act, c, cotg)
        step(i)
        hidden_back(xp, c, slope_x)
        hidden_back(dg, c, slope_d)
        return 0

    lax.fori_loop(0, n_feed, feed_far, 0)

    def back_up(b, put):
        left = gh[blk(b), :]
        tiles(width, lambda c: put(c, dot(left, wup[c, :], 1, 1)))

    sum_sec = Scatter(1, 1)
    sum_sec.far(back_up)
    step(n_feed)
    sum_sec.close(back_up, gmid)
    step(n_feed + 1)
    now = n_feed + 2

    def up_rows(i, _):
        weight_rows(f_cols + i * 256, sec, chunk(i), gh)

        @pl.when(i >= n_up - 3)
        def _():
            step(now + i - (n_up - 3))

        return 0

    lax.fori_loop(0, n_up, up_rows, 0)
    sum_sec.wait()
    now = now + 3

    zero_rows = jnp.zeros((1, width), F32)

    def total(v):
        return jnp.sum(v, axis=0, keepdims=True)

    def middle_back(i, carry):
        d_gain, d_shift, d_out, d_down = carry
        r = pl.ds(pl.multiple_of(i * CH, CH), CH)
        e = gmid[r, :] + sum_sec.extra(r)
        n, scale = norm_parts(mid[r, :])
        tt = e * gain_two
        inner = (tt - jnp.mean(tt, -1, keepdims=True) - n * jnp.mean(tt * n, -1, keepdims=True)) * scale
        c_rows = cotg[pl.ds(pl.multiple_of(t * rows + i * CH, CH), CH), :].astype(F32)
        gm = c_rows + inner
        gmid[r, :] = gm
        low = gm.astype(BF)
        branch[pl.ds(pl.multiple_of(t * rows + i * CH, CH), CH), :] = low
        return (
            d_gain + total(e * n), d_shift + total(e), d_out + total(low.astype(F32)), d_down + total(c_rows)
        )

    d_gain, d_shift, d_out, d_down = lax.fori_loop(0, rows // CH, middle_back, (zero_rows,) * 4)
    small[3:4, :] = d_gain
    small[4:5, :] = d_shift
    small[2:3, :] = d_out
    small[5:6, :] = d_down
    gather_cot.drain()
    gather_branch = Gather(branch, 1)
    gather_branch.start()
    sum_sec.drain()
    step(now)

    def down(b, put):
        left = act[blk(b), :]
        tiles(width, lambda c: put(c, dot(left, wdown[:, c], 1, 0)))

    sum_down = Scatter(0, 0)
    sum_down.far(down, send=False)
    step(now + 1)
    sum_down.close(down, lo)
    load_first = pltpu.make_async_copy(first_h, first2, wsem.at[6])
    load_first.start()
    step(now + 2)
    now = now + 3

    def back_out(b):
        grad = dot(branch[blk(b), :], wout[...], 1, 1).astype(BF)
        for h in range(heads):
            dO[h, blk(b), :] = grad[:, h * HD : (h + 1) * HD]

    back_out(t)
    gather_branch.near()
    back_out(cp)
    gather_branch.far()
    sum_down.send()
    back_out(xp)
    gather_branch.diag()
    back_out(dg)
    paced = gap == 0
    if paced:
        step(now)
        now = now + 1
    else:
        steps(now, start_of(ring))
        now = start_of(ring)
    w_rows = heads * HD
    left = ctxT[...]
    tiles(width, lambda c: part.__setitem__((slice(0, w_rows), c), dot(left, branch[:, c], 1, 0).astype(BF)))

    def attend_back(h, _):
        k = qkv[heads + h]
        v = qkv[2 * heads + h]
        for i in range(LEN // HALF):
            r = slice(i * HALF, (i + 1) * HALF)
            q = qkv[h, r, :]
            o_grad = dO[h, r, :]
            s = dot(k, q, 1, 1) * (SCALE * LOG2E) + bias[:, 0:1]
            p = jnp.exp2(s - lse[h, i])
            dp = dot(v, o_grad, 1, 1)
            delta = jnp.sum(p * dp, axis=0, keepdims=True)
            ds = (p * (dp - delta)).astype(BF)
            d_v = dot(p.astype(BF), o_grad, 1, 0)
            d_k = dot(ds, q, 1, 0)
            if i == 0:
                dv[...] = d_v
                dk[...] = d_k
            else:
                dv[...] = dv[...] + d_v
                dk[...] = dk[...] + d_k
            d_q = dot(kt[h], ds, 1, 0) * SCALE
            qkv[h, r, :] = d_q.T.astype(BF)
        qkv[heads + h] = (dk[...] * SCALE).astype(BF)
        qkv[2 * heads + h] = dv[...].astype(BF)
        if paced:
            step(now + h)
        return 0

    lax.fori_loop(0, heads, attend_back, 0)
    now = now + heads * paced

    def assemble(i, carry):
        r = pl.ds(pl.multiple_of(i * 256, 256), 256)
        for p in range(3 * heads):
            dmx[r, p * HD : (p + 1) * HD] = qkv[p, r, :]
        return carry + total(dmx[r, 0:cols_qkv].astype(F32))

    gather_sec.drain()
    small[7:8, 0:cols_qkv] = lax.fori_loop(0, LEN // 256, assemble, jnp.zeros((1, cols_qkv), F32))

    if paced:
        step(now)
        now = now + 1

    def back_first(b, put):
        left = dmx[blk(b), 0:cols_qkv]
        tiles(width, lambda c: put(c, dot(left, win[:, c], 1, 0)))

    sum_down.drain()
    sum_first = Scatter(1, 1)
    sum_first.far(back_first)
    if paced:
        step(now)
    sum_first.close(back_first, gtok)
    now = now + paced
    load_first.wait()

    def finish_out(i, _):
        r = pl.ds(pl.multiple_of(i * CH, CH), CH)
        lo[r, :] = mid[r, :] + lo[r, :] + sum_down.extra(r) + bias_down
        return 0

    def tokens_back(i, carry):
        d_gain, d_shift = carry
        r = pl.ds(pl.multiple_of(i * CH, CH), CH)
        e = gtok[r, :] + sum_first.extra(r)
        n, scale = norm_parts(tok[r, :].astype(F32))
        tt = e * gain_one
        inner = (tt - jnp.mean(tt, -1, keepdims=True) - n * jnp.mean(tt * n, -1, keepdims=True)) * scale
        gtok[r, :] = gmid[r, :] + inner
        return (d_gain + total(e * n), d_shift + total(e))

    put_lo = pltpu.make_async_copy(lo, lo_h, wsem.at[7])
    put_gtok = pltpu.make_async_copy(gtok, gtok_h, wsem.at[8])
    upto = start_of(ring + w_rows // UNIT)
    assert now <= upto
    steps(now, upto)
    now = upto
    for base in range(0, cols_qkv, 256):
        top = min(base + 256, cols_qkv)
        weight_rows(w_rows + base, dmx, slice(base, top), first2)
        upto = start_of(ring + (w_rows + top) // UNIT - 1) + 1
        steps(now, upto)
        now = upto
        if base == 256:
            sum_first.wait()
            d_gain, d_shift = lax.fori_loop(0, rows // CH, tokens_back, (zero_rows,) * 2)
            small[0:1, :] = d_gain
            small[1:2, :] = d_shift
            put_gtok.start()
        if base == 512:
            sum_down.wait()
            lax.fori_loop(0, rows // CH, finish_out, 0)
            put_lo.start()
    steps(now, last)
    put_lo.wait()
    put_gtok.wait()

    gather_branch.drain()
    sum_first.drain()

    @pl.when(has_up)
    def _():
        s_copy(4, small, smr.at[4], up_dev).wait_send()


def widen(counts, gout, lo, gtok, small, *refs):
    outs, (lo_o, gtok_o), vectors, gb_in = refs[:4], refs[4:6], refs[6:13], refs[13]
    held, full, two, sems = refs[14:]
    tile = 128
    copies = []
    at = 0
    for count, out in zip(counts, outs):
        for start in range(0, count, tile):
            r = slice(at + start, at + min(start + tile, count))
            dst = slice(start, min(start + tile, count))
            copies.append((r, out.at[dst, :]))
        at = at + count
    fetch = [pltpu.make_async_copy(src, two.at[i], sems.at[i]) for i, src in enumerate((lo, gtok))]
    moves = [pltpu.make_async_copy(two.at[i], dst, sems.at[i]) for i, dst in enumerate((lo_o, gtok_o))]
    loads = [
        pltpu.make_async_copy(gout.at[r, :], held.at[r, :], sems.at[2 + 2 * i]) for i, (r, _) in enumerate(copies)
    ]
    stores = [pltpu.make_async_copy(full.at[r, :], out, sems.at[3 + 2 * i]) for i, (r, out) in enumerate(copies)]
    for item in fetch + loads:
        item.start()
    for i, out in enumerate(vectors):
        out[...] = small[i, :]
    cols = gb_in.shape[1]
    gb_in[0:1, :] = small[7:8, 0:cols]
    gb_in[1:2, :] = small[7:8, 2 * cols : 3 * cols]
    for item, move in zip(fetch, moves):
        item.wait()
        move.start()
    for (r, _), load, store in zip(copies, loads, stores):
        load.wait()
        full[r, :] = held[r, :].astype(F32)
        store.start()
    for item in stores + moves:
        item.wait()


def solution(mesh):
    n_dp = mesh.shape["dp"]

    def local(tokens, lengths, gain_one, shift_one, weight_in, bias_in, weight_out, bias_out, gain_two, shift_two,
              weight_up, bias_up, weight_down, bias_down, cotangent):
        rows, width = tokens.shape
        cols = weight_in.shape[2]
        heads = cols // HD
        f_cols = weight_up.shape[1]
        w_in = weight_in.transpose(1, 2, 0).reshape(3 * cols, width)
        total = 4 * rows
        g_rows = f_cols + width + 4 * cols
        ring = (f_cols + width) // UNIT
        vm = pl.BlockSpec(memory_space=pltpu.VMEM)
        hb = pl.BlockSpec(memory_space=pl.ANY)
        big = pltpu.VMEM((total, width), BF)
        lo, gtok, small, gout, _first = pl.pallas_call(
            functools.partial(kernel, n_dp),
            out_shape=[
                jax.ShapeDtypeStruct((rows, width), F32),
                jax.ShapeDtypeStruct((rows, width), F32),
                jax.ShapeDtypeStruct((8, width), F32),
                jax.ShapeDtypeStruct((g_rows, width), BF),
                jax.ShapeDtypeStruct((total, width), BF),
            ],
            in_specs=[pl.BlockSpec(memory_space=pltpu.SMEM), vm, hb] + [vm] * 8 + [hb] * 4,
            out_specs=[hb, hb, vm, hb, hb],
            scratch_shapes=[
                pltpu.VMEM((rows, width), F32),
                pltpu.VMEM((rows, width), F32),
                pltpu.VMEM((3 * cols, width), BF),
                pltpu.VMEM((cols, width), BF),
                pltpu.VMEM((width, f_cols), BF),
                pltpu.VMEM((f_cols, width), BF),
                big, big, big,
                pltpu.VMEM((total, f_cols), BF),
                pltpu.VMEM((total, f_cols), BF),
                pltpu.VMEM((3 * heads, LEN, HD), BF),
                pltpu.VMEM((heads, HD, LEN), BF),
                pltpu.VMEM((heads, HD, LEN), BF),
                pltpu.VMEM((cols, LEN), BF),
                pltpu.VMEM((heads, LEN, HD), BF),
                pltpu.VMEM((LEN, HD), F32),
                pltpu.VMEM((LEN, HD), F32),
                pltpu.VMEM((rows, width), F32),
                pltpu.VMEM((rows, width), F32),
                pltpu.VMEM((LEN, 128), F32),
                pltpu.VMEM((heads, 2, 1, 2 * rows), F32),
                pltpu.VMEM((3, rows, width), BF),
                pltpu.VMEM((2, 3, rows, width), BF),
                pltpu.VMEM((ring * UNIT, width), BF),
                pltpu.VMEM((SLOTS, YH, width), BF),
                pltpu.VMEM((SLOTS, YF, width), BF),
                pltpu.VMEM((SLOTS, YF, width), BF),
                pltpu.VMEM((SLOTS, ZF, width), BF),
                pltpu.VMEM((SLOTS, ZF, width), BF),
                pltpu.VMEM((SLOTS, ZF, width), BF),
                pltpu.VMEM((5, 8, width), F32),
                pltpu.SemaphoreType.DMA((9,)),
                pltpu.SemaphoreType.DMA((2, 5)),
                pltpu.SemaphoreType.DMA((2, 5)),
                pltpu.SemaphoreType.DMA((2, 4)),
                pltpu.SemaphoreType.DMA((2, 4)),
                pltpu.SemaphoreType.DMA((KINDS, SLOTS)),
                pltpu.SemaphoreType.DMA((KINDS, SLOTS)),
                pltpu.SemaphoreType.DMA((SLOTS,)),
                pltpu.SemaphoreType.DMA((5,)),
                pltpu.SemaphoreType.DMA((5,)),
            ],
            compiler_params=pltpu.CompilerParams(
                collective_id=0, has_side_effects=True, vmem_limit_bytes=HIGH
            ),
        )(lengths, tokens, cotangent, gain_one, shift_one, bias_out, gain_two, shift_two, bias_down, bias_up, bias_in,
          w_in, weight_out, weight_up, weight_down)
        flat = jax.ShapeDtypeStruct((width,), F32)
        wide = [f_cols, width, cols, 3 * cols]
        outs = pl.pallas_call(
            functools.partial(widen, wide),
            out_shape=[jax.ShapeDtypeStruct((n, width), F32) for n in wide]
            + [jax.ShapeDtypeStruct((rows, width), F32)] * 2
            + [flat] * 7
            + [jax.ShapeDtypeStruct((2, cols), F32)],
            in_specs=[hb, hb, hb, vm],
            out_specs=[hb] * 6 + [vm] * 8,
            scratch_shapes=[
                pltpu.VMEM((g_rows, width), BF),
                pltpu.VMEM((g_rows, width), F32),
                pltpu.VMEM((2, rows, width), F32),
                pltpu.SemaphoreType.DMA((2 * (g_rows // 128 + 4) + 2,)),
            ],
            compiler_params=pltpu.CompilerParams(vmem_limit_bytes=HIGH),
        )(gout, lo, gtok, small)
        g_down, g_up, g_out, g_in, lo, gtok, gg1, gs1, gb_out, gg2, gs2, gb_down, gb_up, gb_in = outs
        g_in = g_in.reshape(3, cols, width).transpose(2, 0, 1)
        return (lo, gtok, gg1, gs1, g_in, gb_in, g_out, gb_out, gg2, gs2, g_up, gb_up, g_down, gb_down)

    rows2 = P(("dp", "tensor"), None)
    every = P()
    return jax.shard_map(
        local,
        mesh=mesh,
        in_specs=(rows2, P("dp"), every, every, P(None, None, "tensor"), P(None, "tensor"), P("tensor", None), every,
                  every, every, P(None, "tensor"), P("tensor"), P("tensor", None), every, rows2),
        out_specs=(rows2, rows2, every, every, P(None, None, "tensor"), P(None, "tensor"), P("tensor", None), every,
                   every, every, P(None, "tensor"), P("tensor"), P("tensor", None), every),
        check_vma=False,
    )
```

```python
import functools

import jax
import jax.numpy as jnp
from jax import lax
from jax.experimental import pallas as pl
from jax.experimental.pallas import tpu as pltpu
from jax.sharding import PartitionSpec as P

HD = 64
LEN = 1024
BF = jnp.bfloat16
F32 = jnp.float32
MESH = pl.DeviceIdType.MESH
LOG2E = 1.4426950408889634
LN2 = 0.6931471805599453
UNIT = 128
YH = UNIT // 4
YF = UNIT // 8
ZF = UNIT // 4
ZA0 = UNIT // 2
ZB0 = ZA0 + ZF
KINDS = 7
SLOTS = 10
HIGH = 62 * 2**20


def dot(left, right, left_dim, right_dim):
    return lax.dot_general(
        left, right, (((left_dim,), (right_dim,)), ((), ())), preferred_element_type=F32
    )


def norm_parts(rows):
    centre = rows - jnp.mean(rows, axis=-1, keepdims=True)
    scale = lax.rsqrt(jnp.mean(centre * centre, axis=-1, keepdims=True) + 1e-05)
    return centre * scale, scale


def kernel(n_dp, len_ref, tok, cot, gain_1, shift_1, b_out, gain_2, shift_2, b_down, b_up, b_in, win_h, wout_h, wup_h, wdown_h,
           lo_h, gtok_h, small, gout, first_h,
           lo, gtok, win, wout, wup, wdown, first, cotg, sec, act, gh,
           qkv, vt, kt, ctxT, dO, dk, dv, mid, gmid, bias, lse,
           ps, rcv, part, yR, zYA, zYB, zZA, zZB, yZ, smr,
           wsem, ag_s, ag_r, rs_s, rs_r, dp_s, dp_r, out_s, sm_s, sm_r):
    line = n_dp // 2
    width = tok.shape[1]
    rows = tok.shape[0]
    heads = dO.shape[0]
    units = gout.shape[0] // UNIT
    ring = part.shape[0] // UNIT
    gap = max(0, 2 * line + 2 - SLOTS)

    def start_of(u):
        return u + gap * (u // SLOTS)

    small_at = start_of(units - 3)
    last = start_of(units - 1) + 2 * line + 2
    branch = first
    first2 = act
    dmx = sec

    g = lax.axis_index("dp")
    t = lax.axis_index("tensor")
    cp = t + 1 - 2 * lax.rem(t, 2)
    xp = lax.rem(t + 2, 4)
    dg = lax.rem(cp + 2, 4)
    y = lax.rem(g, 2)
    zl = lax.div(g, 2)
    chip = lax.div(t, 2)
    core_dev = (g, cp)
    x_dev = (g, xp)
    y_dev = (g + 1 - 2 * y, t)
    up_dev = (g + 2, t)
    dn_dev = (g - 2, t)
    has_up = zl < line - 1
    has_dn = zl > 0

    def blk(b):
        return pl.ds(pl.multiple_of(b * rows, rows), rows)

    def rcopy(src, dst, s_sem, r_sem, dev):
        return pltpu.make_async_remote_copy(
            src_ref=src, dst_ref=dst, send_sem=s_sem, recv_sem=r_sem, device_id=dev, device_id_type=MESH
        )

    loads = [
        pltpu.make_async_copy(win_h, win, wsem.at[0]),
        pltpu.make_async_copy(wout_h, wout, wsem.at[1]),
        pltpu.make_async_copy(wup_h, wup, wsem.at[2]),
        pltpu.make_async_copy(wdown_h, wdown, wsem.at[3]),
    ]
    own_cot = pltpu.make_async_copy(cot, cotg.at[pl.ds(pl.multiple_of(t * rows, rows), rows), :], wsem.at[4])
    loads[0].start()
    own_cot.start()
    for item in loads[1:]:
        item.start()

    barrier = pltpu.get_barrier_semaphore()
    for dev in (core_dev, x_dev, y_dev):
        pl.semaphore_signal(barrier, inc=1, device_id=dev, device_id_type=MESH)

    @pl.when(has_up)
    def _():
        pl.semaphore_signal(barrier, inc=1, device_id=up_dev, device_id_type=MESH)

    @pl.when(has_dn)
    def _():
        pl.semaphore_signal(barrier, inc=1, device_id=dn_dev, device_id_type=MESH)

    hrows = rows // 2

    def piece_rows(b, i):
        return pl.ds(pl.multiple_of(b * rows + i * hrows, hrows), hrows)

    class Gather:
        def __init__(self, buf, at):
            own = buf.at[blk(t), :]
            self.c = rcopy(own, own, ag_s.at[at, 4], ag_r.at[at, 4], core_dev)
            self.x, self.f = [], []
            for i in range(2):
                mine, theirs = buf.at[piece_rows(t, i), :], buf.at[piece_rows(xp, i), :]
                self.x.append(rcopy(mine, mine, ag_s.at[at, i], ag_r.at[at, i], x_dev))
                self.f.append(rcopy(theirs, theirs, ag_s.at[at, 2 + i], ag_r.at[at, 2 + i], core_dev))

        def start(self):
            self.x[0].start()
            self.x[1].start()
            self.c.start()

        def drain(self):
            for item in self.x + [self.c] + self.f:
                item.wait_send()

        def near(self):
            self.c.wait_recv()

        def far(self):
            for i in range(2):
                self.x[i].wait_recv()
                self.f[i].start()

        def diag(self):
            self.f[0].wait_recv()
            self.f[1].wait_recv()

    class Scatter:
        def __init__(self, at, slot):
            self.own_in, self.x_relay, self.x_in = (rcv.at[slot, i] for i in range(3))
            self.d = rcopy(ps.at[0], rcv.at[slot, 1], rs_s.at[at, 0], rs_r.at[at, 0], core_dev)
            self.x = []
            for i in range(2):
                r = pl.ds(i * hrows, hrows)
                self.x.append(
                    rcopy(ps.at[1, r, :], rcv.at[slot, 2, r, :], rs_s.at[at, 2 + i], rs_r.at[at, 2 + i], x_dev)
                )
            self.c = rcopy(ps.at[2], rcv.at[slot, 0], rs_s.at[at, 1], rs_r.at[at, 1], core_dev)

        def far(self, fn, send=True):
            fn(dg, functools.partial(self.put, 0))
            self.d.start()
            fn(xp, functools.partial(self.put, 1))
            self.d.wait_recv()

            def add(i, _):
                r = pl.ds(pl.multiple_of(i * 64, 64), 64)
                ps[1, r, :] = (ps[1, r, :].astype(F32) + self.x_relay[r, :].astype(F32)).astype(BF)
                return 0

            lax.fori_loop(0, rows // 64, add, 0)
            if send:
                self.send()

        def send(self):
            self.x[0].start()
            self.x[1].start()

        @staticmethod
        def put(slot, cols, value):
            ps[slot, :, cols] = value.astype(BF)

        def close(self, fn, total):
            fn(cp, functools.partial(self.put, 2))
            self.c.start()

            def keep(cols, value):
                total[:, cols] = value

            fn(t, keep)

        def wait(self):
            self.c.wait_recv()
            self.x[0].wait_recv()
            self.x[1].wait_recv()

        def extra(self, r):
            return self.own_in[r, :].astype(F32) + self.x_in[r, :].astype(F32)

        def drain(self):
            for item in [self.d, self.c] + self.x:
                item.wait_send()

    def unit_of(m):
        if gap == 0:
            return (m >= 0) & (m < units), m
        r = lax.rem(m, SLOTS + gap)
        u = lax.div(m, SLOTS + gap) * SLOTS + r
        return (m >= 0) & (r < SLOTS) & (u < units), u

    R_OWN, R_OTHER = (y * YH, YH), ((1 - y) * YH, YH)
    R_YA, R_YB = (y * YH, YF), (y * YH + YF, YF)
    R_ZA, R_ZB = (ZA0, ZF), (ZB0, ZF)

    def at(s, where):
        start, count = where
        return pl.ds(pl.multiple_of(s[0] * UNIT + start, count), count)

    def dcopy(kind, s, src_rows, dst, dev):
        return rcopy(part.at[at(s, src_rows), :], dst, dp_s.at[kind, s[1]], dp_r.at[kind, s[1]], dev)

    def c_y(s):
        return dcopy(0, s, R_OTHER, yR.at[s[1]], y_dev)

    def c_ya(s):
        return dcopy(1, s, R_YA, zYA.at[s[1]], dn_dev)

    def c_yb(s):
        return dcopy(2, s, R_YB, zYB.at[s[1]], up_dev)

    def c_za(s):
        return dcopy(3, s, R_ZA, zZA.at[s[1]], dn_dev)

    def c_zb(s):
        return dcopy(4, s, R_ZB, zZB.at[s[1]], up_dev)

    def c_ex(s, which):
        return dcopy(5, s, which, yZ.at[s[1]], y_dev)

    def b_ya(s):
        return dcopy(1, s, R_YA, zYA.at[s[1]], up_dev)

    def b_yb(s):
        return dcopy(2, s, R_YB, zYB.at[s[1]], dn_dev)

    def b_y(s):
        return dcopy(6, s, R_OWN, part.at[at(s, R_OWN), :], y_dev)

    def b_za(s):
        return dcopy(3, s, R_ZA, zZA.at[s[1]], up_dev)

    def b_zb(s):
        return dcopy(4, s, R_ZB, zZB.at[s[1]], dn_dev)

    def add_in(s, where, got):
        r = at(s, where)
        part[r, :] = (part[r, :].astype(F32) + got[s[1]].astype(F32)).astype(BF)

    def out_copy(s, u):
        return pltpu.make_async_copy(
            part.at[at(s, (0, UNIT)), :], gout.at[pl.ds(pl.multiple_of(u * UNIT, UNIT), UNIT), :], out_s.at[s[1]]
        )

    def on(m, cond, fn):
        ok, u = unit_of(m)
        if cond is not None:
            ok = ok & cond

        @pl.when(ok)
        def _():
            fn((lax.rem(u, ring), lax.rem(u, SLOTS)), u)

    def step(n):
        def begin(s, u):
            c_y(s).start()

            @pl.when(zl == line - 1)
            def _():
                c_za(s).start()

            @pl.when(zl == 0)
            def _():
                c_zb(s).start()

        def pair_sum(s, u):
            c_y(s).wait()
            add_in(s, R_OWN, yR)

            @pl.when(zl == line - 1)
            def _():
                c_ya(s).start()

            @pl.when(zl == 0)
            def _():
                c_yb(s).start()

        def line_zb(s, u):
            c_zb(s).wait_recv()
            add_in(s, R_ZB, zZB)

            @pl.when(has_up)
            def _():
                c_zb(s).start()

            @pl.when(zl == line - 1)
            def _():
                c_ex(s, R_ZB).start()

        def line_za(s, u):
            c_za(s).wait_recv()
            add_in(s, R_ZA, zZA)

            @pl.when(has_dn)
            def _():
                c_za(s).start()

            @pl.when(zl == 0)
            def _():
                c_ex(s, R_ZA).start()

        def pair_za(s, u):
            c_ex(s, R_ZA).wait()
            add_in(s, R_ZA, yZ)
            b_za(s).start()

        def pair_zb(s, u):
            c_ex(s, R_ZB).wait()
            add_in(s, R_ZB, yZ)
            b_zb(s).start()

        def line_yb(s, u):
            c_yb(s).wait_recv()
            add_in(s, R_YB, zYB)

            @pl.when(has_up)
            def _():
                c_yb(s).start()

            @pl.when(zl == line - 1)
            def _():
                b_yb(s).start()

        def line_ya(s, u):
            c_ya(s).wait_recv()
            add_in(s, R_YA, zYA)

            @pl.when(has_dn)
            def _():
                c_ya(s).start()

            @pl.when(zl == 0)
            def _():
                b_ya(s).start()

        def back_a(s, u):
            c_za(s).wait_send()
            c_ya(s).wait_send()
            b_za(s).wait_recv()
            b_ya(s).wait_recv()
            part[at(s, R_ZA), :] = zZA[s[1]]
            part[at(s, R_YA), :] = zYA[s[1]]

            @pl.when(has_up)
            def _():
                b_za(s).start()
                b_ya(s).start()

        def back_b(s, u):
            c_zb(s).wait_send()
            c_yb(s).wait_send()
            b_zb(s).wait_recv()
            b_yb(s).wait_recv()
            part[at(s, R_ZB), :] = zZB[s[1]]
            part[at(s, R_YB), :] = zYB[s[1]]

            @pl.when(has_dn)
            def _():
                b_zb(s).start()
                b_yb(s).start()

        def back_pair(s, u):
            b_y(s).start()

        def finish(s, u):
            b_y(s).wait_recv()
            out_copy(s, u).start()

        def drain(s, u):
            out_copy(s, u).wait()
            b_y(s).wait_send()

            @pl.when(has_up)
            def _():
                for item in (b_ya, b_za):
                    item(s).wait_send()

            @pl.when(has_dn)
            def _():
                for item in (b_yb, b_zb):
                    item(s).wait_send()

        on(n, None, begin)
        on(n - line, zl == 0, pair_za)
        on(n - zl, has_dn, line_zb)
        on(n - (line - 1 - zl), has_up, line_za)
        on(n - 1, None, pair_sum)
        on(n - line, zl == line - 1, pair_zb)
        on(n - 1 - zl, has_dn, line_yb)
        on(n - line + zl, has_up, line_ya)
        on(n - line - zl, has_dn, back_a)
        on(n - line - (line - 1 - zl), has_up, back_b)
        on(n - 2 * line + 1, None, back_pair)
        on(n - 2 * line, None, finish)
        on(n - 2 * line - 1, None, drain)

    shared = lax.broadcasted_iota(jnp.int32, (8, width), 0) < 6

    def s_copy(i, src, dst, dev):
        return rcopy(src, dst, sm_s.at[i], sm_r.at[i], dev)

    def small_step(n):
        core = s_copy(0, small, smr.at[0], core_dev)
        across = s_copy(1, small, smr.at[1], x_dev)
        pair = s_copy(2, small, smr.at[2], y_dev)
        down = s_copy(3, small, smr.at[3], dn_dev)
        back = s_copy(4, small, smr.at[4], up_dev)

        def when(m, cond, fn):
            ok = n == small_at + m
            if cond is not None:
                ok = ok & cond
            pl.when(ok)(fn)

        def s0():
            core.start()

        def s1():
            core.wait()
            small[...] = small[...] + jnp.where(shared, smr[0], 0.0)
            across.start()

        def s2():
            across.wait()
            small[...] = small[...] + jnp.where(shared, smr[1], 0.0)
            pair.start()

        def s3():
            pair.wait()
            small[...] = small[...] + smr[2]

            @pl.when(zl == line - 1)
            def _():
                down.start()

        def s4():
            down.wait_recv()
            small[...] = small[...] + smr[3]

            @pl.when(has_dn)
            def _():
                down.start()

            @pl.when(zl == 0)
            def _():
                back.start()

        def s5():
            back.wait_recv()

            @pl.when(has_dn & (zl > 0))
            def _():
                down.wait_send()

            small[...] = smr[4]

            @pl.when(has_up)
            def _():
                back.start()

        when(0, None, s0)
        when(1, None, s1)
        when(2, None, s2)
        when(3, None, s3)
        when(3 + line - 1 - zl, has_up, s4)
        when(3 + line - 1 + zl, has_dn, s5)

    def steps(lo_n, hi_n):
        def body(n, _):
            step(n)
            small_step(n)
            return 0

        lax.fori_loop(lo_n, hi_n, body, 0)

    keys = lax.broadcasted_iota(jnp.int32, (LEN, 128), 0)
    bias[...] = jnp.where(keys < len_ref[0], 0.0, -1e30)
    gain_one, shift_one = gain_1[...].reshape(1, width), shift_1[...].reshape(1, width)
    gain_two, shift_two = gain_2[...].reshape(1, width), shift_2[...].reshape(1, width)
    bias_out, bias_down = b_out[...].reshape(1, width), b_down[...].reshape(1, width)
    CH = 32

    def norm_one(i, _):
        r = pl.ds(pl.multiple_of(i * CH, CH), CH)
        n, _s = norm_parts(tok[r, :].astype(F32))
        first[pl.ds(pl.multiple_of(t * rows + i * CH, CH), CH), :] = (n * gain_one + shift_one).astype(BF)
        return 0

    gather_first = Gather(first, 0)
    lax.fori_loop(0, hrows // CH, norm_one, 0)
    pl.semaphore_wait(barrier, 3 + has_up.astype(jnp.int32) + has_dn.astype(jnp.int32))
    gather_first.x[0].start()
    lax.fori_loop(hrows // CH, rows // CH, norm_one, 0)
    gather_first.x[1].start()
    gather_first.c.start()
    own_cot.wait()
    gather_cot = Gather(cotg, 1)
    gather_cot.start()
    loads[0].wait()

    cols_qkv = 3 * heads * HD

    def project(b):
        f = first[blk(b), :]
        for base in range(0, cols_qkv, 384):
            w = min(384, cols_qkv - base)
            mixed = dot(f, win[base : base + w, :], 1, 1)
            for i in range(base // HD, (base + w) // HD):
                which, h = i // heads, i % heads
                piece = mixed[:, i * HD - base : (i + 1) * HD - base]
                if which != 1:
                    row = which // 2
                    piece = piece + b_in[row : row + 1, h * HD : (h + 1) * HD]
                piece = piece.astype(BF)
                qkv[i, blk(b), :] = piece
                if which == 1:
                    kt[h, :, blk(b)] = piece.T
                if which == 2:
                    vt[h, :, blk(b)] = piece.T

    project(t)
    gather_first.near()
    project(cp)
    gather_first.far()
    project(xp)
    gather_first.diag()
    project(dg)
    keep_first = pltpu.make_async_copy(first, first_h, wsem.at[5])
    keep_first.start()

    HALF = 2 * rows
    SCALE = HD**-0.5

    def half(i):
        return pl.ds(pl.multiple_of(i * HALF, HALF), HALF)

    def attend(i):
        def head(h, _):
            q = qkv[h, half(i), :]
            k = qkv[heads + h]
            s = dot(k, q, 1, 1) * (SCALE * LOG2E) + bias[:, 0:1]
            top = jnp.max(s, axis=0, keepdims=True)
            p = jnp.exp2(s - top)
            total = jnp.sum(p, axis=0, keepdims=True)
            o = dot(vt[h], p.astype(BF), 1, 0) / total
            ctxT[pl.ds(pl.multiple_of(h * HD, HD), HD), half(i)] = o.astype(BF)
            lse[h, i] = top + jnp.log2(total)
            return 0

        lax.fori_loop(0, heads, head, 0)

    def tiles(n_cols, fn):
        for c0 in range(0, n_cols, 256):
            fn(slice(c0, c0 + 256))

    def project_out(b, put):
        left = ctxT[:, blk(b)]
        tiles(width, lambda c: put(c, dot(left, wout[:, c], 0, 0)))

    loads[1].wait()
    attend(1 - chip)
    sum_out = Scatter(0, 0)
    sum_out.far(project_out)
    attend(chip)
    gather_cot.near()
    gather_cot.far()
    sum_out.close(project_out, mid)
    sum_out.c.wait_recv()
    sum_out.x[0].wait_recv()

    def norm_two(i, _):
        r = pl.ds(pl.multiple_of(i * CH, CH), CH)
        v = tok[r, :].astype(F32) + (mid[r, :] + sum_out.extra(r) + bias_out)
        mid[r, :] = v
        n, _s = norm_parts(v)
        sec[pl.ds(pl.multiple_of(t * rows + i * CH, CH), CH), :] = (n * gain_two + shift_two).astype(BF)
        return 0

    keep_first.wait()
    gather_first.drain()
    gather_sec = Gather(sec, 0)
    lax.fori_loop(0, hrows // CH, norm_two, 0)
    gather_sec.x[0].start()
    sum_out.x[1].wait_recv()
    lax.fori_loop(hrows // CH, rows // CH, norm_two, 0)
    gather_sec.x[1].start()
    gather_sec.c.start()
    sum_out.drain()
    gather_cot.diag()
    loads[2].wait()
    loads[3].wait()

    small[...] = jnp.zeros((8, width), F32)
    f_cols = wup.shape[1]

    def activate(b, c):
        hid = dot(sec[blk(b), :], wup[:, c], 1, 0) + b_up[c].reshape(1, 256)
        phi = 0.5 * (1.0 + lax.erf(hid * 0.7071067811865476))
        act[blk(b), c] = (hid * phi).astype(BF)
        return phi + hid * (0.3989422804014327 * jnp.exp(hid * hid * -0.5))

    def hidden_back(b, c, slope):
        grad = (dot(cotg[blk(b), :], wdown[c, :], 1, 1) * slope).astype(BF)
        gh[blk(b), c] = grad
        small[6:7, c] = small[6:7, c] + jnp.sum(grad.astype(F32), axis=0, keepdims=True)

    def chunk(i):
        return pl.ds(pl.multiple_of(i * 256, 256), 256)

    def feed(b):
        def cols(i, _):
            hidden_back(b, chunk(i), activate(b, chunk(i)))
            return 0

        lax.fori_loop(0, f_cols // 256, cols, 0)

    def weight_rows(base, left, c, right):
        lhs = left[:, c]
        r = pl.ds(pl.multiple_of(base, 64), lhs.shape[1])
        tiles(width, lambda cc: part.__setitem__((r, cc), dot(lhs, right[:, cc], 0, 0).astype(BF)))

    feed(t)
    gather_sec.near()
    feed(cp)
    gather_sec.far()
    gather_sec.diag()

    n_feed = f_cols // 256
    n_up = width // 256

    def feed_far(i, _):
        c = chunk(i)
        slope_x, slope_d = activate(xp, c), activate(dg, c)
        weight_rows(i * 256, act, c, cotg)
        step(i)
        hidden_back(xp, c, slope_x)
        hidden_back(dg, c, slope_d)
        return 0

    lax.fori_loop(0, n_feed, feed_far, 0)

    def back_up(b, put):
        left = gh[blk(b), :]
        tiles(width, lambda c: put(c, dot(left, wup[c, :], 1, 1)))

    sum_sec = Scatter(1, 1)
    sum_sec.far(back_up)
    step(n_feed)
    sum_sec.close(back_up, gmid)
    step(n_feed + 1)
    now = n_feed + 2

    def up_rows(i, _):
        weight_rows(f_cols + i * 256, sec, chunk(i), gh)

        @pl.when(i >= n_up - 3)
        def _():
            step(now + i - (n_up - 3))

        return 0

    lax.fori_loop(0, n_up, up_rows, 0)
    sum_sec.c.wait_recv()
    sum_sec.x[0].wait_recv()
    now = now + 3

    zero_rows = jnp.zeros((1, width), F32)

    def total(v):
        return jnp.sum(v, axis=0, keepdims=True)

    def middle_back(i, carry):
        d_gain, d_shift, d_out, d_down = carry
        r = pl.ds(pl.multiple_of(i * CH, CH), CH)
        e = gmid[r, :] + sum_sec.extra(r)
        n, scale = norm_parts(mid[r, :])
        tt = e * gain_two
        inner = (tt - jnp.mean(tt, -1, keepdims=True) - n * jnp.mean(tt * n, -1, keepdims=True)) * scale
        c_rows = cotg[pl.ds(pl.multiple_of(t * rows + i * CH, CH), CH), :].astype(F32)
        gm = c_rows + inner
        gmid[r, :] = gm
        low = gm.astype(BF)
        branch[pl.ds(pl.multiple_of(t * rows + i * CH, CH), CH), :] = low
        return (
            d_gain + total(e * n), d_shift + total(e), d_out + total(low.astype(F32)), d_down + total(c_rows)
        )

    gather_cot.drain()
    gather_branch = Gather(branch, 1)
    carry = lax.fori_loop(0, hrows // CH, middle_back, (zero_rows,) * 4)
    gather_branch.x[0].start()
    sum_sec.x[1].wait_recv()
    d_gain, d_shift, d_out, d_down = lax.fori_loop(hrows // CH, rows // CH, middle_back, carry)
    small[3:4, :] = d_gain
    small[4:5, :] = d_shift
    small[2:3, :] = d_out
    small[5:6, :] = d_down
    gather_branch.x[1].start()
    gather_branch.c.start()
    sum_sec.drain()
    step(now)

    def down(b, put):
        left = act[blk(b), :]
        tiles(width, lambda c: put(c, dot(left, wdown[:, c], 1, 0)))

    sum_down = Scatter(0, 0)
    sum_down.far(down, send=False)
    step(now + 1)
    sum_down.close(down, lo)
    load_first = pltpu.make_async_copy(first_h, first2, wsem.at[6])
    load_first.start()
    step(now + 2)
    now = now + 3

    def back_out(b):
        grad = dot(branch[blk(b), :], wout[...], 1, 1).astype(BF)
        for h in range(heads):
            dO[h, blk(b), :] = grad[:, h * HD : (h + 1) * HD]

    back_out(t)
    gather_branch.near()
    back_out(cp)
    gather_branch.far()
    sum_down.send()
    back_out(xp)
    gather_branch.diag()
    back_out(dg)
    paced = gap == 0
    if paced:
        step(now)
        now = now + 1
    else:
        steps(now, start_of(ring))
        now = start_of(ring)
    w_rows = heads * HD
    left = ctxT[...]
    tiles(width, lambda c: part.__setitem__((slice(0, w_rows), c), dot(left, branch[:, c], 1, 0).astype(BF)))

    def attend_back(h, _):
        k = qkv[heads + h]
        v = qkv[2 * heads + h]
        for i in range(LEN // HALF):
            r = slice(i * HALF, (i + 1) * HALF)
            q = qkv[h, r, :]
            o_grad = dO[h, r, :]
            s = dot(k, q, 1, 1) * (SCALE * LOG2E) + bias[:, 0:1]
            p = jnp.exp2(s - lse[h, i])
            dp = dot(v, o_grad, 1, 1)
            delta = jnp.sum(p * dp, axis=0, keepdims=True)
            ds = (p * (dp - delta)).astype(BF)
            d_v = dot(p.astype(BF), o_grad, 1, 0)
            d_k = dot(ds, q, 1, 0)
            if i == 0:
                dv[...] = d_v
                dk[...] = d_k
            else:
                dv[...] = dv[...] + d_v
                dk[...] = dk[...] + d_k
            d_q = dot(kt[h], ds, 1, 0) * SCALE
            qkv[h, r, :] = d_q.T.astype(BF)
        qkv[heads + h] = (dk[...] * SCALE).astype(BF)
        qkv[2 * heads + h] = dv[...].astype(BF)
        if paced:
            step(now + h)
        return 0

    lax.fori_loop(0, heads, attend_back, 0)
    now = now + heads * paced

    def assemble(i, carry):
        r = pl.ds(pl.multiple_of(i * 256, 256), 256)
        for p in range(3 * heads):
            dmx[r, p * HD : (p + 1) * HD] = qkv[p, r, :]
        return carry + total(dmx[r, 0:cols_qkv].astype(F32))

    gather_sec.drain()
    small[7:8, 0:cols_qkv] = lax.fori_loop(0, LEN // 256, assemble, jnp.zeros((1, cols_qkv), F32))

    if paced:
        step(now)
        now = now + 1

    def back_first(b, put):
        left = dmx[blk(b), 0:cols_qkv]
        tiles(width, lambda c: put(c, dot(left, win[:, c], 1, 0)))

    sum_down.drain()
    sum_first = Scatter(1, 1)
    sum_first.far(back_first)
    if paced:
        step(now)
    sum_first.close(back_first, gtok)
    now = now + paced
    load_first.wait()

    def finish_out(i, _):
        r = pl.ds(pl.multiple_of(i * CH, CH), CH)
        lo[r, :] = mid[r, :] + lo[r, :] + sum_down.extra(r) + bias_down
        return 0

    def tokens_back(i, carry):
        d_gain, d_shift = carry
        r = pl.ds(pl.multiple_of(i * CH, CH), CH)
        e = gtok[r, :] + sum_first.extra(r)
        n, scale = norm_parts(tok[r, :].astype(F32))
        tt = e * gain_one
        inner = (tt - jnp.mean(tt, -1, keepdims=True) - n * jnp.mean(tt * n, -1, keepdims=True)) * scale
        gtok[r, :] = gmid[r, :] + inner
        return (d_gain + total(e * n), d_shift + total(e))

    put_lo = pltpu.make_async_copy(lo, lo_h, wsem.at[7])
    put_gtok = pltpu.make_async_copy(gtok, gtok_h, wsem.at[8])
    upto = start_of(ring + w_rows // UNIT)
    assert now <= upto
    steps(now, upto)
    now = upto
    for base in range(0, cols_qkv, 256):
        top = min(base + 256, cols_qkv)
        weight_rows(w_rows + base, dmx, slice(base, top), first2)
        upto = start_of(ring + (w_rows + top) // UNIT - 1) + 1
        steps(now, upto)
        now = upto
        if base == 256:
            sum_first.wait()
            d_gain, d_shift = lax.fori_loop(0, rows // CH, tokens_back, (zero_rows,) * 2)
            small[0:1, :] = d_gain
            small[1:2, :] = d_shift
            put_gtok.start()
        if base == 512:
            sum_down.wait()
            lax.fori_loop(0, rows // CH, finish_out, 0)
            put_lo.start()
    steps(now, last)
    put_lo.wait()
    put_gtok.wait()

    gather_branch.drain()
    sum_first.drain()

    @pl.when(has_up)
    def _():
        s_copy(4, small, smr.at[4], up_dev).wait_send()


def widen(counts, gout, lo, gtok, small, *refs):
    outs, (lo_o, gtok_o), vectors, gb_in = refs[:4], refs[4:6], refs[6:13], refs[13]
    held, full, two, sems = refs[14:]
    tile = 128
    copies = []
    at = 0
    for count, out in zip(counts, outs):
        for start in range(0, count, tile):
            r = slice(at + start, at + min(start + tile, count))
            dst = slice(start, min(start + tile, count))
            copies.append((r, out.at[dst, :]))
        at = at + count
    fetch = [pltpu.make_async_copy(src, two.at[i], sems.at[i]) for i, src in enumerate((lo, gtok))]
    moves = [pltpu.make_async_copy(two.at[i], dst, sems.at[i]) for i, dst in enumerate((lo_o, gtok_o))]
    loads = [
        pltpu.make_async_copy(gout.at[r, :], held.at[r, :], sems.at[2 + 2 * i]) for i, (r, _) in enumerate(copies)
    ]
    stores = [pltpu.make_async_copy(full.at[r, :], out, sems.at[3 + 2 * i]) for i, (r, out) in enumerate(copies)]
    for item in fetch + loads:
        item.start()
    for i, out in enumerate(vectors):
        out[...] = small[i, :]
    cols = gb_in.shape[1]
    gb_in[0:1, :] = small[7:8, 0:cols]
    gb_in[1:2, :] = small[7:8, 2 * cols : 3 * cols]
    for item, move in zip(fetch, moves):
        item.wait()
        move.start()
    for (r, _), load, store in zip(copies, loads, stores):
        load.wait()
        full[r, :] = held[r, :].astype(F32)
        store.start()
    for item in stores + moves:
        item.wait()


def solution(mesh):
    n_dp = mesh.shape["dp"]

    def local(tokens, lengths, gain_one, shift_one, weight_in, bias_in, weight_out, bias_out, gain_two, shift_two,
              weight_up, bias_up, weight_down, bias_down, cotangent):
        rows, width = tokens.shape
        cols = weight_in.shape[2]
        heads = cols // HD
        f_cols = weight_up.shape[1]
        w_in = weight_in.transpose(1, 2, 0).reshape(3 * cols, width)
        total = 4 * rows
        g_rows = f_cols + width + 4 * cols
        ring = (f_cols + width) // UNIT
        vm = pl.BlockSpec(memory_space=pltpu.VMEM)
        hb = pl.BlockSpec(memory_space=pl.ANY)
        big = pltpu.VMEM((total, width), BF)
        lo, gtok, small, gout, _first = pl.pallas_call(
            functools.partial(kernel, n_dp),
            out_shape=[
                jax.ShapeDtypeStruct((rows, width), F32),
                jax.ShapeDtypeStruct((rows, width), F32),
                jax.ShapeDtypeStruct((8, width), F32),
                jax.ShapeDtypeStruct((g_rows, width), BF),
                jax.ShapeDtypeStruct((total, width), BF),
            ],
            in_specs=[pl.BlockSpec(memory_space=pltpu.SMEM), vm, hb] + [vm] * 8 + [hb] * 4,
            out_specs=[hb, hb, vm, hb, hb],
            scratch_shapes=[
                pltpu.VMEM((rows, width), F32),
                pltpu.VMEM((rows, width), F32),
                pltpu.VMEM((3 * cols, width), BF),
                pltpu.VMEM((cols, width), BF),
                pltpu.VMEM((width, f_cols), BF),
                pltpu.VMEM((f_cols, width), BF),
                big, big, big,
                pltpu.VMEM((total, f_cols), BF),
                pltpu.VMEM((total, f_cols), BF),
                pltpu.VMEM((3 * heads, LEN, HD), BF),
                pltpu.VMEM((heads, HD, LEN), BF),
                pltpu.VMEM((heads, HD, LEN), BF),
                pltpu.VMEM((cols, LEN), BF),
                pltpu.VMEM((heads, LEN, HD), BF),
                pltpu.VMEM((LEN, HD), F32),
                pltpu.VMEM((LEN, HD), F32),
                pltpu.VMEM((rows, width), F32),
                pltpu.VMEM((rows, width), F32),
                pltpu.VMEM((LEN, 128), F32),
                pltpu.VMEM((heads, 2, 1, 2 * rows), F32),
                pltpu.VMEM((3, rows, width), BF),
                pltpu.VMEM((2, 3, rows, width), BF),
                pltpu.VMEM((ring * UNIT, width), BF),
                pltpu.VMEM((SLOTS, YH, width), BF),
                pltpu.VMEM((SLOTS, YF, width), BF),
                pltpu.VMEM((SLOTS, YF, width), BF),
                pltpu.VMEM((SLOTS, ZF, width), BF),
                pltpu.VMEM((SLOTS, ZF, width), BF),
                pltpu.VMEM((SLOTS, ZF, width), BF),
                pltpu.VMEM((5, 8, width), F32),
                pltpu.SemaphoreType.DMA((9,)),
                pltpu.SemaphoreType.DMA((2, 5)),
                pltpu.SemaphoreType.DMA((2, 5)),
                pltpu.SemaphoreType.DMA((2, 4)),
                pltpu.SemaphoreType.DMA((2, 4)),
                pltpu.SemaphoreType.DMA((KINDS, SLOTS)),
                pltpu.SemaphoreType.DMA((KINDS, SLOTS)),
                pltpu.SemaphoreType.DMA((SLOTS,)),
                pltpu.SemaphoreType.DMA((5,)),
                pltpu.SemaphoreType.DMA((5,)),
            ],
            compiler_params=pltpu.CompilerParams(
                collective_id=0, has_side_effects=True, vmem_limit_bytes=HIGH
            ),
        )(lengths, tokens, cotangent, gain_one, shift_one, bias_out, gain_two, shift_two, bias_down, bias_up, bias_in,
          w_in, weight_out, weight_up, weight_down)
        flat = jax.ShapeDtypeStruct((width,), F32)
        wide = [f_cols, width, cols, 3 * cols]
        outs = pl.pallas_call(
            functools.partial(widen, wide),
            out_shape=[jax.ShapeDtypeStruct((n, width), F32) for n in wide]
            + [jax.ShapeDtypeStruct((rows, width), F32)] * 2
            + [flat] * 7
            + [jax.ShapeDtypeStruct((2, cols), F32)],
            in_specs=[hb, hb, hb, vm],
            out_specs=[hb] * 6 + [vm] * 8,
            scratch_shapes=[
                pltpu.VMEM((g_rows, width), BF),
                pltpu.VMEM((g_rows, width), F32),
                pltpu.VMEM((2, rows, width), F32),
                pltpu.SemaphoreType.DMA((2 * (g_rows // 128 + 4) + 2,)),
            ],
            compiler_params=pltpu.CompilerParams(vmem_limit_bytes=HIGH),
        )(gout, lo, gtok, small)
        g_down, g_up, g_out, g_in, lo, gtok, gg1, gs1, gb_out, gg2, gs2, gb_down, gb_up, gb_in = outs
        g_in = g_in.reshape(3, cols, width).transpose(2, 0, 1)
        return (lo, gtok, gg1, gs1, g_in, gb_in, g_out, gb_out, gg2, gs2, g_up, gb_up, g_down, gb_down)

    rows2 = P(("dp", "tensor"), None)
    every = P()
    return jax.shard_map(
        local,
        mesh=mesh,
        in_specs=(rows2, P("dp"), every, every, P(None, None, "tensor"), P(None, "tensor"), P("tensor", None), every,
                  every, every, P(None, "tensor"), P("tensor"), P("tensor", None), every, rows2),
        out_specs=(rows2, rows2, every, every, P(None, None, "tensor"), P(None, "tensor"), P("tensor", None), every,
                   every, every, P(None, "tensor"), P("tensor"), P("tensor", None), every),
        check_vma=False,
    )
```
